32 devices in a mesh: rep: 8 (over y, x, core), shard: 4 (over z).
Axes of the slice: x: 2, y: 2, z: 4, core: 2. Of those that a mesh axis runs over, the one named last changes fastest.
Arguments:
- hidden_in: bfloat16 [16384, 1024], P(('rep', 'shard')), may hold values from -6 to 6
- segment_ids: int32 [16384], P(('rep', 'shard')), may hold values from 0 to 63, never falling along the last dimension, each value on 1 to 1024 neighbouring positions
- norm_gains: float32 [2, 1024], P(None, 'shard'), may hold values from 0.1 to 1.9
- w_mix_in: bfloat16 [1024, 6144], P('shard'), may hold values from -0.1875 to 0.1875
- w_decay: bfloat16 [1024, 16], P('shard'), may hold values from -0.1875 to 0.1875
- decay_params: float32 [2, 8], P(None, 'shard'), may hold values from -4 to 1
- conv_weight: float32 [4, 4096], P(None, 'shard'), may hold values from -3 to 3
- out_gain: float32 [256], P('shard'), may hold values from 0.1 to 1.9
- w_mix_out: bfloat16 [2048, 1024], P('shard'), may hold values from -0.25 to 0.25
- w_gate_up: bfloat16 [1024, 5632], P('shard'), may hold values from -0.1875 to 0.1875
- w_down: bfloat16 [2816, 1024], P('shard'), may hold values from -0.21875 to 0.21875
- cotangent: bfloat16 [16384, 1024], P(('rep', 'shard')), may hold values from -6 to 6
Outputs:
- hidden_out: bfloat16 [16384, 1024], P(('rep', 'shard'))
- grad_in: float32 [16384, 1024], P(('rep', 'shard'))
- grad_norm_gains: float32 [2, 1024], P(None, 'shard')
- grad_mix_in: float32 [1024, 6144], P('shard')
- grad_decay: float32 [1024, 16], P('shard')
- grad_decay_params: float32 [2, 8], P(None, 'shard')
- grad_conv: float32 [4, 4096], P(None, 'shard')
- grad_out_gain: float32 [256], P('shard')
- grad_mix_out: float32 [2048, 1024], P('shard')
- grad_gate_up: float32 [1024, 5632], P('shard')
- grad_down: float32 [2816, 1024], P('shard')
The draws below stay inside these ranges and needn't reach their ends.
Inputs may be any that keep to these rules, and one draw needn't show every extreme that they name: `segment_ids`: document numbers never fall along the tokens; every document holds 1 to 1024 tokens and one holds exactly 1024; a document may run across the end of a sequence, where the state starts afresh.
All inputs are finite; a program needn't handle non-finite values.
Results may differ from the reference program's by a relative error of at most 0.023.
Values may be sent and summed in bfloat16 or wider, within the bound.
No kernel may reach another device: no remote copies, remote signals or barrier semaphores. Data moves between devices by JAX's collectives and lax.ppermute only.
A program may use at most 384 MiB of HBM per device.

```python
import math
import jax
import jax.numpy as jnp
import numpy as np
from jax import lax

D = 1024
HEADS = 8
DK = 128
DV = 256
FF = 2816
CONV = 4
SPAN = 64
SEQ = 512
KEYS = 1024
VALS = 2048
CHANNELS = 4096
PROJ = 6144
TOKENS = 16384
DOCS = 64
DOC_MOST = 1024


def block_levels(own_key, extent, split, smallest, largest):
    factor_of, own = 1.0, jax.random.fold_in(own_key, 6)
    for axis_at, parts in split:
        heights = jnp.exp(jax.random.uniform(jax.random.fold_in(own, axis_at), (parts,), jnp.float32, smallest / len(split), largest / len(split)))
        factor_of = factor_of * jnp.repeat(heights, extent[axis_at] // parts).reshape([-1 if axis == axis_at else 1 for axis in range(len(extent))])
    return factor_of


def profile(count, total, limit, slope):
    weights = [(1 << 20) // math.isqrt(standing ** slope) + 1 for standing in range(2, count + 1)]
    rest, holding = total - limit - (count - 1), [1] * (count - 1)
    while rest > 0:
        candidates = [i for i in range(count - 1) if holding[i] < limit]
        mass, remaining = sum([weights[i] for i in candidates]), rest
        for i in candidates:
            extra = min(limit - holding[i], max(1, remaining * weights[i] // mass), rest)
            holding[i] = holding[i] + extra
            rest = rest - extra
    return np.array([limit] + holding)


def ragged_sizes(rng, amount, total, reach, skew):
    if amount == 2:
        one = jax.random.randint(rng, (), max(1, total - reach), min(reach, total - 1) + 1)
        return jnp.stack([one, total - one])
    tallies = jnp.asarray(profile(amount, total, reach, skew), jnp.int32)
    pairs = (amount - 1) // 2
    source_of, receiver = tallies[1:1 + 2 * pairs:2], tallies[2:2 + 2 * pairs:2]
    slack = jnp.minimum(source_of - 1, reach - receiver)
    moved = jax.random.randint(jax.random.fold_in(rng, 1), (pairs,), 0, 1 << 20) % (slack + 1)
    tallies = tallies.at[1:1 + 2 * pairs:2].set(source_of - moved).at[2:2 + 2 * pairs:2].set(receiver + moved)
    return tallies[jax.random.permutation(jax.random.fold_in(rng, 2), amount)]


def noise(rng, extent, spread, bound, cuts=(), held_as=jnp.bfloat16):
    entries = spread * jax.random.normal(rng, extent, jnp.float32)
    if cuts:
        entries = entries * block_levels(rng, extent, cuts, -0.22, 0.18)
    return jnp.clip(entries, -bound, bound).astype(held_as)


def setup_inputs(seed: int = 0) -> dict:
    seeds = jax.random.split(jax.random.key(seed), 13)
    return {
        "hidden_in": noise(seeds[0], (TOKENS, D), 1.0, 6.0, ((0, 32),)),
        "segment_ids": jnp.searchsorted(jnp.cumsum(ragged_sizes(seeds[1], DOCS, TOKENS, DOC_MOST, 1)), jnp.arange(TOKENS), side="right").astype(jnp.int32),
        "norm_gains": jnp.clip(1.0 + 0.18 * jax.random.normal(seeds[2], (2, D), jnp.float32), 0.1, 1.9),
        "w_mix_in": noise(seeds[3], (D, PROJ), D ** -0.5, 0.1875, ((0, 4),)),
        "w_decay": noise(seeds[4], (D, 2 * HEADS), D ** -0.5, 0.1875, ((0, 4),)),
        "decay_params": jnp.clip(-4.0 + 5.0 * jax.random.uniform(seeds[5], (2, HEADS), jnp.float32) ** block_levels(seeds[5], (2, HEADS), ((1, 4),), -0.2, 0.2), -4.0, 1.0),
        "conv_weight": noise(seeds[6], (CONV, CHANNELS), CONV ** -0.5, 3.0, ((1, 4),), jnp.float32),
        "out_gain": jnp.clip(1.0 + 0.18 * jax.random.normal(seeds[7], (DV,), jnp.float32), 0.1, 1.9),
        "w_mix_out": noise(seeds[8], (VALS, D), (VALS // 4) ** -0.5, 0.25, ((0, 4),)),
        "w_gate_up": noise(seeds[9], (D, 2 * FF), D ** -0.5, 0.1875, ((0, 4),)),
        "w_down": noise(seeds[10], (FF, D), (FF // 4) ** -0.5, 0.21875, ((0, 4),)),
        "cotangent": noise(seeds[11], (TOKENS, D), 1.0, 6.0, ((0, 32),)),
    }


HIGHEST = lax.Precision.HIGHEST
epsilon = 1e-06
out_floor = 0.01

@jax.custom_vjp
def low(v):
    return lax.optimization_barrier(v.astype(jnp.bfloat16)).astype(jnp.float32)

@jax.custom_vjp
def low_back(v):
    return v

def low_keep(v):
    return (low(v), None)

def low_pass(kept, grad):
    return (grad,)

def back_keep(v):
    return (v, None)

def back_low(kept, grad):
    return (low(grad),)
low.defvjp(low_keep, low_pass)
low_back.defvjp(back_keep, back_low)

def rms_scale(values, gain):
    return values * lax.rsqrt(lax.optimization_barrier(jnp.mean(values * values, axis=-1, keepdims=True)) + epsilon) * gain

def product(left, right):
    return jnp.einsum('...i,ij->...j', left, right, precision=HIGHEST)

def delayed(values, shift):
    widths = [(0, 0)] * values.ndim
    widths[-2] = (shift, 0)
    return jnp.pad(values, widths)[..., :values.shape[-2], :]

def delayed_ids(segments, shift):
    widths = [(0, 0)] * segments.ndim
    widths[-1] = (shift, 0)
    return jnp.pad(segments, widths, constant_values=-1)[..., :segments.shape[-1]]

def prepare(projected, decay_logits, segments, decay_params, conv_weight):
    channels = 2 * KEYS + VALS
    mixed = projected[..., :channels]
    gate_raw = projected[..., channels:]
    total = conv_weight[0] * mixed
    for shift in range(1, CONV):
        match = (delayed_ids(segments, shift) == segments).astype(jnp.float32)[..., None]
        total = total + conv_weight[shift] * delayed(mixed, shift) * match
    active = jax.nn.silu(total)
    leading = active.shape[:-1]
    queries = active[..., :KEYS].reshape(leading + (HEADS, DK))
    keys_raw = active[..., KEYS:2 * KEYS].reshape(leading + (HEADS, DK))
    keys_unit = keys_raw * lax.rsqrt(lax.optimization_barrier(jnp.sum(keys_raw * keys_raw, axis=-1, keepdims=True)) + epsilon)
    values = active[..., 2 * KEYS:].reshape(leading + (HEADS, DV))
    beta = jax.nn.sigmoid(decay_logits[..., HEADS:])
    gamma = -jnp.exp(decay_params[0]) * jax.nn.softplus(decay_logits[..., :HEADS] + decay_params[1])
    return (queries, keys_unit, values, beta, gamma, gate_raw)

def finish(outputs, gate_raw, out_gain):
    normed = outputs * lax.rsqrt(lax.optimization_barrier(jnp.mean(outputs * outputs, axis=-1, keepdims=True)) + out_floor) * out_gain
    return normed.reshape(gate_raw.shape) * jax.nn.silu(gate_raw)

def token_step(carry, inputs):
    state, previous = carry
    queries, keys_unit, values, beta, gamma, segments = inputs
    alive = (segments == previous).astype(jnp.float32)
    decayed = state * (jnp.exp(gamma) * alive[:, None])[..., None, None]
    predicted = jnp.einsum('bhvd,bhd->bhv', decayed, keys_unit, precision=HIGHEST)
    update = beta[..., None] * (values - predicted)
    state = decayed + update[..., :, None] * keys_unit[..., None, :]
    output = jnp.einsum('bhvd,bhd->bhv', state, queries, precision=HIGHEST)
    return ((state, segments), output)

def block_scan(carry, block):
    return lax.scan(token_step, carry, block)

def delta_rule(queries, keys_unit, values, beta, gamma, segments):
    batch, length = segments.shape
    blocks = length // SPAN

    def timewise(array):
        moved = jnp.moveaxis(array, 1, 0)
        return moved.reshape((blocks, SPAN) + moved.shape[1:])
    inputs = (timewise(queries), timewise(keys_unit), timewise(values), timewise(beta), timewise(gamma), timewise(segments))
    state = jnp.zeros((batch, HEADS, DV, DK), jnp.float32)
    previous = jnp.full((batch,), -1, jnp.int32)
    carry, outputs = lax.scan(jax.checkpoint(block_scan), (state, previous), inputs)
    outputs = outputs.reshape((length, batch, HEADS, DV))
    return jnp.moveaxis(outputs, 0, 1)

def layer(hidden, segments, weights):
    gains, w_in, w_dec, dparams, conv_w, gain_out, w_out, w_gu, w_dn = weights
    normed_one = low(rms_scale(hidden, gains[0]))
    projected = low_back(product(normed_one, w_in))
    decay_logits = low_back(product(normed_one, w_dec))
    queries, keys_unit, values, beta, gamma, gate_raw = prepare(projected, decay_logits, segments, dparams, conv_w)
    outputs = delta_rule(low(queries), low(keys_unit), low(values), beta, gamma, segments)
    mixed_out = low(finish(outputs, gate_raw, gain_out))
    residual = hidden + low_back(product(mixed_out, w_out))
    normed_two = low(rms_scale(residual, gains[1]))
    gate_up = low_back(product(normed_two, w_gu))
    inner = low(jax.nn.silu(gate_up[..., :FF]) * gate_up[..., FF:])
    return residual + low_back(product(inner, w_dn))

def reference(hidden_in, segment_ids, norm_gains, w_mix_in, w_decay, decay_params, conv_weight, out_gain, w_mix_out, w_gate_up, w_down, cotangent):
    weights = (norm_gains.astype(jnp.float32), w_mix_in.astype(jnp.float32), w_decay.astype(jnp.float32), decay_params.astype(jnp.float32), conv_weight.astype(jnp.float32), out_gain.astype(jnp.float32), w_mix_out.astype(jnp.float32), w_gate_up.astype(jnp.float32), w_down.astype(jnp.float32))
    count = TOKENS // SEQ
    group = math.gcd(count, max(1, 4096 // SEQ))
    rounds = count // group
    hidden = hidden_in.astype(jnp.float32).reshape(rounds, group, SEQ, D)
    segments = segment_ids.reshape(rounds, group, SEQ)
    incoming = cotangent.astype(jnp.float32).reshape(rounds, group, SEQ, D)

    def one_group(totals, inputs):
        block_hidden, block_segments, block_grad = inputs

        def apply(values, params):
            return layer(values, block_segments, params)
        output, pullback = jax.vjp(apply, block_hidden, weights)
        grad_hidden, grad_weights = pullback(block_grad)
        totals = jax.tree.map(jnp.add, totals, grad_weights)
        return (totals, (output, grad_hidden))
    zeros = jax.tree.map(jnp.zeros_like, weights)
    totals, results = lax.scan(one_group, zeros, (hidden, segments, incoming))
    outputs, grads = results
    return (outputs.reshape(TOKENS, D).astype(jnp.bfloat16), grads.reshape(TOKENS, D), totals[0], totals[1], totals[2], totals[3], totals[4], totals[5], totals[6], totals[7], totals[8])
```

```python
import functools

import jax
import jax.numpy as jnp
from jax import lax
from jax.experimental import pallas as pl
from jax.experimental.pallas import tpu as pltpu
from jax.sharding import PartitionSpec as P

HEADS = 8
DK = 128
DV = 256
FF = 2816
CONV = 4
KEYS = 1024
VALS = 2048
CHUNK = 128
epsilon = 1e-06
out_floor = 0.01
BF = jnp.bfloat16
F32 = jnp.float32


def dot_nn(a, b):
    return jnp.dot(a, b, preferred_element_type=F32)


def dot_nt(a, b):
    return lax.dot_general(a, b, (((1,), (1,)), ((), ())), preferred_element_type=F32)


def dot_tn(a, b):
    return lax.dot_general(a, b, (((0,), (0,)), ((), ())), preferred_element_type=F32)


def twice(x):
    return jnp.concatenate([x, x], axis=1)


def sigmoid(x):
    return 1.0 / (1.0 + jnp.exp(-x))


def column(row):
    return jnp.broadcast_to(row, (CHUNK, CHUNK)).T


def fill_masks(seg_ref, mask_ref):
    rows = seg_ref.shape[0]
    seg = seg_ref[...]
    at = lax.broadcasted_iota(jnp.int32, seg.shape, 0)
    for shift in range(1, CONV):
        match = (pltpu.roll(seg, shift, 0) == seg) & (at >= shift)
        mask_ref[shift - 1] = match.astype(F32)


def fill_sums(gamma_ref, sums_ref):
    lane = lax.broadcasted_iota(jnp.int32, (HEADS, CHUNK), 1)
    for c in range(gamma_ref.shape[1] // CHUNK):
        span = pl.ds(c * CHUNK, CHUNK)
        total = gamma_ref[:, span]
        step = 1
        while step < CHUNK:
            total = total + jnp.where(lane >= step, pltpu.roll(total, step, 1), 0.0)
            step *= 2
        for i in range(HEADS):
            sums_ref[i, :, span] = total[i : i + 1]


def wide(mask, columns):
    return mask if columns == CHUNK else twice(mask)


def convolve(x, taps, mask_ref):
    total = x * taps[0:1]
    for shift in range(1, CONV):
        total = total + pltpu.roll(x, shift, 0) * (wide(mask_ref[shift - 1], x.shape[1]) * taps[shift : shift + 1])
    return total


def inverses(systems):
    row = lax.broadcasted_iota(jnp.int32, (CHUNK, CHUNK), 0)
    col = lax.broadcasted_iota(jnp.int32, (CHUNK, CHUNK), 1)
    eye = (row == col).astype(F32)
    near = (row // 2) == (col // 2)
    found = [eye - jnp.where(near, a, 0.0) for a in systems]
    size = 2
    while size < CHUNK:
        part = ((row // (2 * size)) == (col // (2 * size))) & ((row // size) != (col // size))
        packed = [x.astype(BF) for x in found]
        inner = [dot_nn(jnp.where(part, a, 0.0).astype(BF), x).astype(BF) for a, x in zip(systems, packed)]
        found = [x - dot_nn(p, i) for x, p, i in zip(found, packed, inner)]
        size *= 2
    return [x.astype(BF) for x in found]


def chunk_scales(c, h, sums_ref, beta_ref, seg_ref, segrow_ref):
    span = pl.ds(c * CHUNK, CHUNK)
    seg = seg_ref[span, :]
    segrow = segrow_ref[0:1, span]
    sums = sums_ref[h, :, span]
    beta = column(beta_ref[0, :, span])
    down = column(sums)
    row = lax.broadcasted_iota(jnp.int32, (CHUNK, CHUNK), 0)
    col = lax.broadcasted_iota(jnp.int32, (CHUNK, CHUNK), 1)
    same = seg == segrow
    decays = jnp.exp(jnp.where(same & (row >= col), down - sums, -1e30))
    strict = jnp.where(row > col, decays, 0.0)
    ends = jnp.exp(jnp.where(seg == seg[CHUNK - 1 : CHUNK], down[CHUNK - 1 : CHUNK] - down, -1e30))
    if c:
        before = seg_ref[c * CHUNK - 1 : c * CHUNK, :]
        reach = jnp.where(seg == before, jnp.exp(down), 0.0)
    else:
        reach = None
    return beta, decays, strict, ends, reach


def mix_kernel(
    q_ref, k_ref, v_ref, gate_ref, seg_ref, segrow_ref, gamma_ref, beta_ref,
    tapq_ref, tapk_ref, tapv_ref, gain_ref,
    mixed_ref, out_ref, fresh_ref, inv_ref, state_ref,
    mask_ref, sums_ref,
):
    h = pl.program_id(0)

    @pl.when(h == 0)
    def _():
        fill_masks(seg_ref, mask_ref)
        fill_sums(gamma_ref, sums_ref)

    rows = q_ref.shape[0]
    chunks = rows // CHUNK

    def active(ref, tap_ref):
        total = convolve(ref[...].astype(F32), tap_ref[...], mask_ref)
        return total * sigmoid(total)

    q = active(q_ref, tapq_ref).astype(BF)
    kraw = active(k_ref, tapk_ref)
    k = (kraw * lax.rsqrt(jnp.sum(kraw * kraw, axis=-1, keepdims=True) + epsilon)).astype(BF)
    v = active(v_ref, tapv_ref).astype(BF)
    cut = lambda x, c: x[c * CHUNK : (c + 1) * CHUNK]
    scales = [chunk_scales(c, h, sums_ref, beta_ref, seg_ref, segrow_ref) for c in range(chunks)]
    systems = []
    attend = []
    for c in range(chunks):
        beta, decays, strict, ends, reach = scales[c]
        systems.append(beta * strict * dot_nt(cut(k, c), cut(k, c)))
        attend.append((decays * dot_nt(cut(q, c), cut(k, c))).astype(BF))
    found = inverses(systems)
    state = None
    for c in range(chunks):
        beta, decays, strict, ends, reach = scales[c]
        kc, qc, vc = cut(k, c), cut(q, c), cut(v, c).astype(F32)
        inv_ref[0, c] = found[c]
        if c:
            packed = state.astype(BF)
            state_ref[0, c] = packed
            right = twice(beta) * (vc - twice(reach) * dot_nn(kc, packed))
        else:
            state_ref[0, c] = jnp.zeros((DK, DV), BF)
            right = twice(beta) * vc
        fresh = dot_nn(found[c], right.astype(BF)).astype(BF)
        fresh_ref[c * CHUNK : (c + 1) * CHUNK, :] = fresh
        out = dot_nn(attend[c], fresh)
        if c:
            out = out + twice(reach) * dot_nn(qc, packed)
        if c < chunks - 1:
            grown = dot_tn((ends * kc.astype(F32)).astype(BF), fresh)
            state = grown + twice(reach[CHUNK - 1 : CHUNK]) * state if c else grown
        out_ref[c * CHUNK : (c + 1) * CHUNK, :] = out
        unit = out * lax.rsqrt(jnp.mean(out * out, axis=-1, keepdims=True) + out_floor)
        gate = gate_ref[c * CHUNK : (c + 1) * CHUNK, :].astype(F32)
        mixed_ref[c * CHUNK : (c + 1) * CHUNK, :] = (unit * gain_ref[...] * (gate * sigmoid(gate))).astype(BF)


def whole(shape):
    return pl.BlockSpec(shape, lambda h: (0,) * len(shape))


def per_head(rows):
    return pl.BlockSpec((1, 1, rows), lambda h: (h, 0, 0))


def mixer(projected, seg, segrow, gamma, beta, taps, gain):
    rows = projected.shape[0]
    chunks = rows // CHUNK
    return pl.pallas_call(
        mix_kernel,
        grid=(HEADS,),
        in_specs=[
            pl.BlockSpec((rows, DK), lambda h: (0, h)),
            pl.BlockSpec((rows, DK), lambda h: (0, HEADS + h)),
            pl.BlockSpec((rows, DV), lambda h: (0, HEADS + h)),
            pl.BlockSpec((rows, DV), lambda h: (0, 2 * HEADS + h)),
            whole((rows, CHUNK)), whole((8, rows)), whole((HEADS, rows)), per_head(rows),
            pl.BlockSpec((CONV, DK), lambda h: (0, h)),
            pl.BlockSpec((CONV, DK), lambda h: (0, HEADS + h)),
            pl.BlockSpec((CONV, DV), lambda h: (0, HEADS + h)),
            whole((1, DV)),
        ],
        out_specs=[
            pl.BlockSpec((rows, DV), lambda h: (0, h)),
            pl.BlockSpec((rows, DV), lambda h: (0, h)),
            pl.BlockSpec((rows, DV), lambda h: (0, h)),
            pl.BlockSpec((1, chunks, CHUNK, CHUNK), lambda h: (h, 0, 0, 0)),
            pl.BlockSpec((1, chunks, DK, DV), lambda h: (h, 0, 0, 0)),
        ],
        out_shape=[
            jax.ShapeDtypeStruct((rows, VALS), BF),
            jax.ShapeDtypeStruct((rows, VALS), F32),
            jax.ShapeDtypeStruct((rows, VALS), BF),
            jax.ShapeDtypeStruct((HEADS, chunks, CHUNK, CHUNK), BF),
            jax.ShapeDtypeStruct((HEADS, chunks, DK, DV), BF),
        ],
        scratch_shapes=[pltpu.VMEM((CONV - 1, rows, CHUNK), F32), pltpu.VMEM((HEADS, 1, rows), F32)],
        compiler_params=pltpu.CompilerParams(vmem_limit_bytes=48 * 2**20),
        cost_estimate=pl.CostEstimate(flops=int(3e10), bytes_accessed=int(3e7), transcendentals=0),
    )(projected, projected, projected, projected, seg, segrow, gamma, beta[:, None], taps, taps, taps, gain)


def back_kernel(
    q_ref, k_ref, v_ref, gate_ref, seg_ref, segrow_ref, gamma_ref, beta_ref,
    tapq_ref, tapk_ref, tapv_ref, gain_ref, out_ref, fresh_ref, inv_ref, state_ref, back_ref,
    dq_ref, dk_ref, dv_ref, dgate_ref, dtapq_ref, dtapk_ref, dtapv_ref, dgain_ref, dgamma_ref, dbeta_ref,
    mask_ref, sums_ref, lift_ref,
):
    h = pl.program_id(0)

    @pl.when(h == 0)
    def _():
        fill_masks(seg_ref, mask_ref)
        fill_sums(gamma_ref, sums_ref)
        dgain_ref[...] = jnp.zeros_like(dgain_ref)

    rows = q_ref.shape[0]
    chunks = rows // CHUNK

    def active(ref, tap_ref):
        total = convolve(ref[...].astype(F32), tap_ref[...], mask_ref)
        s = sigmoid(total)
        return total * s, s * (1.0 + total * (1.0 - s))

    qf, qslope = active(q_ref, tapq_ref)
    kraw, kslope = active(k_ref, tapk_ref)
    vf, vslope = active(v_ref, tapv_ref)
    kscale = lax.rsqrt(jnp.sum(kraw * kraw, axis=-1, keepdims=True) + epsilon)
    kunit = kraw * kscale
    q, k, v = qf.astype(BF), kunit.astype(BF), vf.astype(BF)
    cut = lambda x, c: x[c * CHUNK : (c + 1) * CHUNK]
    gain = gain_ref[...]
    carried = None
    dqs, dks, dvs = [None] * chunks, [None] * chunks, [None] * chunks
    dgain = jnp.zeros((1, DV), F32)
    for c in reversed(range(chunks)):
        span = pl.ds(c * CHUNK, CHUNK)
        beta, decays, strict, ends, reach = chunk_scales(c, h, sums_ref, beta_ref, seg_ref, segrow_ref)
        kc, qc, vc = cut(k, c), cut(q, c), cut(v, c).astype(F32)
        kcf, qcf = kc.astype(F32), qc.astype(F32)
        out, gate, back = out_ref[span, :], gate_ref[span, :].astype(F32), back_ref[span, :].astype(F32)
        p = lax.rsqrt(jnp.mean(out * out, axis=-1, keepdims=True) + out_floor)
        z = out * p
        s = sigmoid(gate)
        a = back * (gate * s)
        az = a * z
        dgain = dgain + jnp.sum(az, axis=0, keepdims=True)
        dgate_ref[span, :] = (back * (z * gain) * (s * (1.0 + gate * (1.0 - s)))).astype(BF)
        dout = p * (a * gain - z * jnp.mean(az * gain, axis=-1, keepdims=True))
        doutb = dout.astype(BF)
        key_key = dot_nt(kc, kc)
        query_key = dot_nt(qc, kc)
        attend = (decays * query_key).astype(BF)
        fresh = fresh_ref[span, :]
        found = inv_ref[0, c]
        dfresh = dot_tn(attend, doutb)
        if carried is not None:
            carriedb = carried.astype(BF)
            dfresh = dfresh + twice(ends) * dot_nn(kc, carriedb)
        dscore = decays * dot_nt(doutb, fresh)
        dright = dot_tn(found, dfresh.astype(BF))
        drightb = dright.astype(BF)
        dsystem = dot_nt(drightb, fresh)
        dvs[c] = twice(beta) * dright
        m = key_key * (strict * dsystem)
        dkk = (beta * strict) * dsystem
        tally = query_key * dscore - beta * m
        dscoreb = dscore.astype(BF)
        dq = dot_nn(dscoreb, kc)
        dk = dot_tn(dscoreb, qc) - dot_nn((dkk + dkk.T).astype(BF), kc)
        side = tally
        edge = None
        if carried is not None:
            dkf = dot_nt((twice(ends) * fresh.astype(F32)).astype(BF), carriedb)
            dk = dk + dkf
            moved = kcf * dkf
            side = side - moved
            edge = jnp.sum(moved, axis=0, keepdims=True)
        if c:
            state = state_ref[0, c]
            rout = (twice(reach) * dout).astype(BF)
            given = dot_nn(kc, state)
            drest = dright * (vc - twice(reach) * given)
            w = (-twice(beta * reach) * dright).astype(BF)
            dqs1 = dot_nt(rout, state)
            dks1 = dot_nt(w, state)
            dq = dq + dqs1
            dk = dk + dks1
            side = side + qcf * dqs1 + kcf * dks1
            grown = dot_tn(jnp.concatenate([qc, kc], axis=0), jnp.concatenate([rout, w], axis=0))
            if carried is not None:
                last = reach[CHUNK - 1 : CHUNK]
                kept = carried * state.astype(F32)
                edge = edge + last * jnp.sum(kept[:, :CHUNK] + kept[:, CHUNK:], axis=0, keepdims=True)
                carried = twice(last) * carried + grown
            else:
                carried = grown
        else:
            drest = dright * vc
        dqs[c] = dq
        dks[c] = dk
        dbeta = drest[:, :CHUNK] + drest[:, CHUNK:] - m
        dbeta_ref[0, :, span] = jnp.sum(dbeta.T, axis=0, keepdims=True)
        lift = jnp.sum(side.T - tally, axis=0, keepdims=True)
        if edge is not None:
            lane = lax.broadcasted_iota(jnp.int32, (1, CHUNK), 1)
            lift = lift + jnp.where(lane == CHUNK - 1, jnp.sum(edge, axis=1, keepdims=True), 0.0)
        lift_ref[h, :, span] = lift
    dgain_ref[...] += dgain

    def spread(grad, ref, tap_ref, to_ref, dtap_ref):
        x, taps = ref[...].astype(F32), tap_ref[...]
        total = grad * taps[0:1]
        sums = [jnp.sum(grad * x, axis=0, keepdims=True)]
        for shift in range(1, CONV):
            masked = grad * wide(mask_ref[shift - 1], x.shape[1])
            sums.append(jnp.sum(masked * pltpu.roll(x, shift, 0), axis=0, keepdims=True))
            total = total + pltpu.roll(masked, rows - shift, 0) * taps[shift : shift + 1]
        to_ref[...] = total.astype(BF)
        dtap_ref[...] = jnp.concatenate(sums, axis=0)

    spread(jnp.concatenate(dqs, axis=0) * qslope, q_ref, tapq_ref, dq_ref, dtapq_ref)
    dk = jnp.concatenate(dks, axis=0)
    dk = kscale * (dk - kunit * jnp.sum(kunit * dk, axis=-1, keepdims=True))
    spread(dk * kslope, k_ref, tapk_ref, dk_ref, dtapk_ref)
    spread(jnp.concatenate(dvs, axis=0) * vslope, v_ref, tapv_ref, dv_ref, dtapv_ref)

    @pl.when(h == HEADS - 1)
    def _():
        lane = lax.broadcasted_iota(jnp.int32, (HEADS, CHUNK), 1)
        for c in range(chunks):
            span = pl.ds(c * CHUNK, CHUNK)
            total = jnp.concatenate([lift_ref[i, :, span] for i in range(HEADS)], axis=0)
            step = 1
            while step < CHUNK:
                total = total + jnp.where(lane < CHUNK - step, pltpu.roll(total, CHUNK - step, 1), 0.0)
                step *= 2
            dgamma_ref[:, span] = total


def mixer_back(projected, seg, segrow, gamma, beta, taps, gain, out, fresh, inv, state, back):
    rows = projected.shape[0]
    chunks = rows // CHUNK
    cols = lambda width, at: pl.BlockSpec((rows, width), lambda h: (0, at + h))
    tap = lambda width, at: pl.BlockSpec((CONV, width), lambda h: (0, at + h))
    return pl.pallas_call(
        back_kernel,
        grid=(HEADS,),
        in_specs=[
            cols(DK, 0), cols(DK, HEADS), cols(DV, HEADS), cols(DV, 2 * HEADS),
            whole((rows, CHUNK)), whole((8, rows)), whole((HEADS, rows)), per_head(rows),
            tap(DK, 0), tap(DK, HEADS), tap(DV, HEADS), whole((1, DV)),
            cols(DV, 0), cols(DV, 0),
            pl.BlockSpec((1, chunks, CHUNK, CHUNK), lambda h: (h, 0, 0, 0)),
            pl.BlockSpec((1, chunks, DK, DV), lambda h: (h, 0, 0, 0)),
            cols(DV, 0),
        ],
        out_specs=[
            cols(DK, 0), cols(DK, 0), cols(DV, 0), cols(DV, 0),
            tap(DK, 0), tap(DK, 0), tap(DV, 0),
            whole((1, DV)), whole((HEADS, rows)), per_head(rows),
        ],
        out_shape=[
            jax.ShapeDtypeStruct((rows, KEYS), BF),
            jax.ShapeDtypeStruct((rows, KEYS), BF),
            jax.ShapeDtypeStruct((rows, VALS), BF),
            jax.ShapeDtypeStruct((rows, VALS), BF),
            jax.ShapeDtypeStruct((CONV, KEYS), F32),
            jax.ShapeDtypeStruct((CONV, KEYS), F32),
            jax.ShapeDtypeStruct((CONV, VALS), F32),
            jax.ShapeDtypeStruct((1, DV), F32),
            jax.ShapeDtypeStruct((HEADS, rows), F32),
            jax.ShapeDtypeStruct((HEADS, 1, rows), F32),
        ],
        scratch_shapes=[
            pltpu.VMEM((CONV - 1, rows, CHUNK), F32),
            pltpu.VMEM((HEADS, 1, rows), F32),
            pltpu.VMEM((HEADS, 1, rows), F32),
        ],
        compiler_params=pltpu.CompilerParams(vmem_limit_bytes=56 * 2**20),
        cost_estimate=pl.CostEstimate(flops=int(6e10), bytes_accessed=int(4e7), transcendentals=0),
    )(projected, projected, projected, projected, seg, segrow, gamma, beta[:, None], taps, taps, taps, gain, out, fresh, inv, state, back)


SHIFTS = (1, 2, 3)


def place():
    rep = lax.axis_index("rep")
    core, x, y = rep % 2, (rep // 2) % 2, (rep // 4) % 2
    a = jnp.where(core == 0, x, y)
    b = jnp.where(core == 0, y, x)
    return core, a, b


def hop(value, kind):
    count = lax.axis_size("rep")
    if kind == "core":
        pairs = [(i, i ^ 1) for i in range(count)]
    elif kind == "first":
        pairs = [(i, i ^ (4 if i & 1 else 2)) for i in range(count)]
    elif kind == "second":
        pairs = [(i, i ^ (2 if i & 1 else 4)) for i in range(count)]
    else:
        pairs = [(i, i ^ kind) for i in range(count)]
    return lax.ppermute(value, "rep", pairs)


def shift(value, by):
    count = lax.axis_size("shard")
    return lax.ppermute(value, "shard", [(i, (i + by) % count) for i in range(count)])


def assemble_kernel(along, size, rows, at_ref, *refs):
    own, pieces, whole_ref = refs[0], refs[1:-1], refs[-1]
    whole_ref[pl.ds(pl.multiple_of(at_ref[0] * rows, 16), rows), :] = own[...]
    for n, piece in enumerate(pieces):
        block, part = at_ref[1 + 2 * n], at_ref[2 + 2 * n]
        if along == 0:
            whole_ref[pl.ds(pl.multiple_of(block * rows + part * size, 16), size), :] = piece[...]
        else:
            whole_ref[pl.ds(pl.multiple_of(block * rows, 16), rows), pl.ds(pl.multiple_of(part * size, 128), size)] = piece[...]


def gather(weight, along):
    core, a, b = place()
    z = lax.axis_index("shard")
    count = lax.axis_size("shard")
    size = weight.shape[along] // 8
    rows = weight.shape[0]
    part = core * 4 + a * 2 + b
    other = (1 - core) * 4 + b * 2 + a
    mine = lax.dynamic_slice_in_dim(weight, part * size, size, along)
    at, pieces = [z], []
    for by in range(1, count):
        block = (z - by) % count
        here = shift(mine, by)
        token = here
        first = hop(here, "first")
        found = [(here, 0), (first, 2), (hop(here, "second"), 1), (hop(first, "second"), 3)]
        for piece, flip in found:
            pieces += [piece, hop(piece, "core")]
            at += [block, part ^ flip, block, other ^ flip]
    full = pl.pallas_call(
        functools.partial(assemble_kernel, along, size, rows),
        in_specs=[pl.BlockSpec(memory_space=pltpu.SMEM)] + [pl.BlockSpec(memory_space=pltpu.VMEM)] * (len(pieces) + 1),
        out_specs=pl.BlockSpec(memory_space=pltpu.VMEM),
        compiler_params=pltpu.CompilerParams(vmem_limit_bytes=48 * 2**20),
        out_shape=jax.ShapeDtypeStruct((rows * count, weight.shape[1]), BF),
    )(jnp.stack(at).astype(jnp.int32), weight, *pieces)
    return full, token


def pick(value, at, size, axis):
    return lax.dynamic_slice_in_dim(value, at * size, size, axis)


def join(bit, mine, theirs, axis):
    return jnp.where(bit == 0, jnp.concatenate([mine, theirs], axis), jnp.concatenate([theirs, mine], axis))


def reduce_grad(left, right):
    core, a, b = place()
    z = lax.axis_index("shard")
    count = lax.axis_size("shard")
    columns = right.shape[1]
    half, quarter = columns // 2, columns // 4
    rows = left.shape[1] // count
    got = hop(dot_tn(left, pick(right, 1 - core, half, 1)).astype(BF), "core")
    own = pick(right, core, half, 1)
    sent = dot_tn(left, pick(own, 1 - a, quarter, 1)) + pick(got, 1 - a, quarter, 1).astype(F32)
    got_first = hop(sent.astype(BF), "first")
    kept = dot_tn(left, pick(own, a, quarter, 1)) + pick(got, a, quarter, 1).astype(F32) + got_first.astype(F32)
    kept = kept.astype(BF).reshape(count, rows, quarter)
    axis = 2 if quarter % 256 == 0 else 1
    size = kept.shape[axis] // 2
    kept = (pick(kept, b, size, axis).astype(F32) + hop(pick(kept, 1 - b, size, axis), "second").astype(F32)).astype(BF)
    extra = 8
    while extra < lax.axis_size("rep"):
        kept = (kept.astype(F32) + hop(kept, extra).astype(F32)).astype(BF)
        extra *= 2
    total = pick(kept, z, 1, 0)[0].astype(F32)
    for by in range(1, count):
        total = total + shift(pick(kept, (z + by) % count, 1, 0)[0], by).astype(F32)
    done = total.astype(BF)
    done = join(b, done, hop(done, "second"), axis - 1)
    done = join(a, done, hop(done, "first"), 1)
    return join(core, done, hop(done, "core"), 1).astype(F32)


def rms_scale(values, gain):
    return values * lax.rsqrt(jnp.mean(values * values, axis=-1, keepdims=True) + epsilon) * gain


def swiglu(gate_up):
    return jax.nn.silu(gate_up[..., :FF]) * gate_up[..., FF:]


def after(value, *others):
    return lax.optimization_barrier((value,) + others)[0]


def share_small(arrays):
    count = lax.axis_size("shard")
    z = lax.axis_index("shard")
    flat = jnp.concatenate([x.astype(F32).reshape(-1) for x in arrays])
    flat = jnp.pad(flat, (0, -flat.shape[0] % 1024)).reshape(1, -1, 128)
    every = jnp.zeros((count,) + flat.shape[1:], F32)
    every = lax.dynamic_update_slice_in_dim(every, flat, z, 0)
    for by in range(1, count):
        every = lax.dynamic_update_slice_in_dim(every, shift(flat, by), (z - by) % count, 0)
    every = every.reshape(count, -1)
    found, start = [], 0
    for x in arrays:
        found.append(every[:, start : start + x.size].reshape((count,) + x.shape))
        start += x.size
    return found


def beside(blocks):
    return jnp.concatenate(list(blocks), axis=-1)


def body(
    hidden_in,
    segment_ids,
    norm_gains,
    w_mix_in,
    w_decay,
    decay_params,
    conv_weight,
    out_gain,
    w_mix_out,
    w_gate_up,
    w_down,
    cotangent,
):
    rows = hidden_in.shape[0]
    z = lax.axis_index("shard")
    small = share_small([norm_gains, decay_params, conv_weight, out_gain[None], w_decay])
    gains, rates, taps, gain_row = (beside(x) for x in small[:4])
    decay_full = small[4].reshape(-1, 2 * HEADS).astype(BF)
    mix_in, token = gather(w_mix_in, 1)
    mix_out, token = gather(after(w_mix_out, token), 1)
    gate_up_full, token = gather(after(w_gate_up, token), 0)
    down_full, token = gather(after(w_down, token), 1)

    hidden = hidden_in.astype(F32)
    normed_one_f, norm_one_pull = jax.vjp(rms_scale, hidden, gains[0])
    normed_one = normed_one_f.astype(BF)
    projected = dot_nn(normed_one, mix_in)
    logits = dot_nt(decay_full.T, normed_one)
    rate, bias = jnp.exp(rates[0])[:, None], rates[1][:, None]
    gamma = -rate * jax.nn.softplus(logits[:HEADS] + bias)
    beta = jax.nn.sigmoid(logits[HEADS:])
    seg = jnp.broadcast_to(segment_ids[:, None], (rows, CHUNK))
    segrow = jnp.broadcast_to(segment_ids[None], (8, rows))
    mixed_out, out, fresh, inv, state = mixer(projected, seg, segrow, gamma, beta, taps, gain_row)
    residual = hidden + dot_nn(mixed_out, mix_out)
    normed_two_f, norm_two_pull = jax.vjp(rms_scale, residual, gains[1])
    normed_two = normed_two_f.astype(BF)
    gate_up = dot_nn(normed_two, gate_up_full)
    inner_f, inner_pull = jax.vjp(swiglu, gate_up)
    inner = inner_f.astype(BF)
    result = (residual + dot_nn(inner, down_full)).astype(BF)
    inner_back = dot_nt(cotangent, down_full)
    (gate_up_grad,) = inner_pull(inner_back)
    gate_up_back = gate_up_grad.astype(BF)
    grad_down = reduce_grad(inner, cotangent)
    grad_gate_up = reduce_grad(normed_two, gate_up_back)
    normed_two_back = dot_nt(gate_up_back, gate_up_full)
    residual_part, gain_two = norm_two_pull(normed_two_back)
    residual_back = cotangent.astype(F32) + residual_part
    branch_back = residual_back.astype(BF)
    mixed_back = dot_nt(branch_back, mix_out)
    grad_mix_out = reduce_grad(mixed_out, branch_back)
    dq, dk, dv, dgate, dtq, dtk, dtv, dgain, dgamma, dbeta = mixer_back(
        projected, seg, segrow, gamma, beta, taps, gain_row, out, fresh, inv, state, mixed_back
    )
    dbeta = dbeta[:, 0]
    projected_back = jnp.concatenate([dq, dk, dv, dgate], axis=1)
    slope = -dgamma * rate * jax.nn.sigmoid(logits[:HEADS] + bias)
    logits_back = jnp.concatenate([slope, dbeta * beta * (1.0 - beta)], axis=0).astype(BF)
    grad_rates = jnp.stack([jnp.sum(dgamma * gamma, axis=1), jnp.sum(slope, axis=1)])
    grad_decay = lax.dot_general(normed_one, logits_back, (((0,), (1,)), ((), ())), preferred_element_type=F32)
    normed_one_back = dot_nt(projected_back, mix_in) + lax.dot_general(
        logits_back, decay_full, (((0,), (1,)), ((), ())), preferred_element_type=F32
    )
    grad_mix_in = reduce_grad(normed_one, projected_back)
    hidden_part, gain_one = norm_one_pull(normed_one_back)
    grad_in = residual_back + hidden_part

    parts = [jnp.stack([gain_one, gain_two]), grad_decay, grad_rates, jnp.concatenate([dtq, dtk, dtv], axis=1), dgain]
    flat = jnp.concatenate([x.reshape(-1) for x in parts])
    flat = jnp.pad(flat, (0, -flat.shape[0] % 1024)).reshape(-1, 128)
    flat = lax.psum(flat, ("rep", "shard")).reshape(-1)
    found, start = [], 0
    for x in parts:
        found.append(flat[start : start + x.size].reshape(x.shape))
        start += x.size
    count = lax.axis_size("shard")
    mine = lambda x, axis: lax.dynamic_slice_in_dim(x, z * (x.shape[axis] // count), x.shape[axis] // count, axis)
    return (
        result,
        grad_in,
        mine(found[0], 1),
        grad_mix_in,
        mine(found[1], 0),
        mine(found[2], 1),
        mine(found[3], 1),
        mine(found[4][0], 0),
        grad_mix_out,
        grad_gate_up,
        grad_down,
    )


def solution(mesh):
    rows, columns, both = P("shard", None), P(None, "shard"), P(("rep", "shard"), None)
    return jax.shard_map(
        body,
        mesh=mesh,
        in_specs=(both, P(("rep", "shard")), columns, rows, rows, columns, columns, P("shard"), rows, rows, rows, both),
        out_specs=(both, both, columns, rows, rows, columns, columns, P("shard"), rows, rows, rows),
        check_vma=False,
    )
```

```python
import functools
import math

import jax
import jax.numpy as jnp
from jax import lax
from jax.experimental import pallas as pl
from jax.experimental.pallas import tpu as pltpu
from jax.sharding import PartitionSpec as P

HEADS = 8
DK = 128
DV = 256
FF = 2816
CONV = 4
KEYS = 1024
VALS = 2048
CHUNK = 128
epsilon = 1e-06
out_floor = 0.01
BF = jnp.bfloat16
F32 = jnp.float32


def dot_nn(a, b):
    return jnp.dot(a, b, preferred_element_type=F32)


def dot_nt(a, b):
    return lax.dot_general(a, b, (((1,), (1,)), ((), ())), preferred_element_type=F32)


def dot_tn(a, b):
    return lax.dot_general(a, b, (((0,), (0,)), ((), ())), preferred_element_type=F32)


def twice(x):
    return jnp.concatenate([x, x], axis=1)


def sigmoid(x):
    return 1.0 / (1.0 + jnp.exp(-x))


def column(row):
    return jnp.broadcast_to(row, (CHUNK, CHUNK)).T


def fill_masks(seg_ref, mask_ref):
    rows = seg_ref.shape[0]
    seg = seg_ref[...]
    at = lax.broadcasted_iota(jnp.int32, seg.shape, 0)
    for shift in range(1, CONV):
        match = (pltpu.roll(seg, shift, 0) == seg) & (at >= shift)
        mask_ref[shift - 1] = match.astype(F32)


def fill_sums(gamma_ref, sums_ref):
    lane = lax.broadcasted_iota(jnp.int32, (gamma_ref.shape[0], CHUNK), 1)
    for c in range(gamma_ref.shape[1] // CHUNK):
        span = pl.ds(c * CHUNK, CHUNK)
        total = gamma_ref[:, span]
        step = 1
        while step < CHUNK:
            total = total + jnp.where(lane >= step, pltpu.roll(total, step, 1), 0.0)
            step *= 2
        for i in range(gamma_ref.shape[0]):
            sums_ref[i, :, span] = total[i : i + 1]


def wide(mask, columns):
    return mask if columns == CHUNK else twice(mask)


def convolve(x, taps, mask_ref):
    total = x * taps[0:1]
    for shift in range(1, CONV):
        total = total + pltpu.roll(x, shift, 0) * (wide(mask_ref[shift - 1], x.shape[1]) * taps[shift : shift + 1])
    return total


def inverses(systems):
    row = lax.broadcasted_iota(jnp.int32, (CHUNK, CHUNK), 0)
    col = lax.broadcasted_iota(jnp.int32, (CHUNK, CHUNK), 1)
    eye = (row == col).astype(F32)
    near = (row // 2) == (col // 2)
    found = [eye - jnp.where(near, a, 0.0) for a in systems]
    size = 2
    while size < CHUNK:
        part = ((row // (2 * size)) == (col // (2 * size))) & ((row // size) != (col // size))
        packed = [x.astype(BF) for x in found]
        inner = [dot_nn(jnp.where(part, a, 0.0).astype(BF), x).astype(BF) for a, x in zip(systems, packed)]
        found = [x - dot_nn(p, i) for x, p, i in zip(found, packed, inner)]
        size *= 2
    return [x.astype(BF) for x in found]


def chunk_scales(c, h, sums_ref, beta_ref, seg_ref, segrow_ref):
    span = pl.ds(c * CHUNK, CHUNK)
    seg = seg_ref[span, :]
    segrow = segrow_ref[0:1, span]
    sums = sums_ref[h, :, span]
    beta = column(beta_ref[0, :, span])
    down = column(sums)
    row = lax.broadcasted_iota(jnp.int32, (CHUNK, CHUNK), 0)
    col = lax.broadcasted_iota(jnp.int32, (CHUNK, CHUNK), 1)
    same = seg == segrow
    decays = jnp.exp(jnp.where(same & (row >= col), down - sums, -1e30))
    strict = jnp.where(row > col, decays, 0.0)
    ends = jnp.exp(jnp.where(seg == seg[CHUNK - 1 : CHUNK], down[CHUNK - 1 : CHUNK] - down, -1e30))
    if c:
        before = seg_ref[c * CHUNK - 1 : c * CHUNK, :]
        reach = jnp.where(seg == before, jnp.exp(down), 0.0)
    else:
        reach = None
    return beta, decays, strict, ends, reach


def mix_kernel(
    q_ref, k_ref, v_ref, gate_ref, seg_ref, segrow_ref, gamma_ref, beta_ref,
    tapq_ref, tapk_ref, tapv_ref, gain_ref,
    mixed_ref, out_ref, fresh_ref, inv_ref, state_ref,
    mask_ref, sums_ref,
):
    h = pl.program_id(0)

    @pl.when(h == 0)
    def _():
        fill_masks(seg_ref, mask_ref)
        fill_sums(gamma_ref, sums_ref)

    rows = q_ref.shape[0]
    chunks = rows // CHUNK

    def active(ref, tap_ref):
        total = convolve(ref[...].astype(F32), tap_ref[...], mask_ref)
        return total * sigmoid(total)

    q = active(q_ref, tapq_ref).astype(BF)
    kraw = active(k_ref, tapk_ref)
    k = (kraw * lax.rsqrt(jnp.sum(kraw * kraw, axis=-1, keepdims=True) + epsilon)).astype(BF)
    v = active(v_ref, tapv_ref).astype(BF)
    cut = lambda x, c: x[c * CHUNK : (c + 1) * CHUNK]
    scales = [chunk_scales(c, h, sums_ref, beta_ref, seg_ref, segrow_ref) for c in range(chunks)]
    systems = []
    attend = []
    for c in range(chunks):
        beta, decays, strict, ends, reach = scales[c]
        systems.append(beta * strict * dot_nt(cut(k, c), cut(k, c)))
        attend.append((decays * dot_nt(cut(q, c), cut(k, c))).astype(BF))
    found = inverses(systems)
    state = None
    for c in range(chunks):
        beta, decays, strict, ends, reach = scales[c]
        kc, qc, vc = cut(k, c), cut(q, c), cut(v, c).astype(F32)
        inv_ref[0, c] = found[c]
        if c:
            packed = state.astype(BF)
            state_ref[0, c] = packed
            right = twice(beta) * (vc - twice(reach) * dot_nn(kc, packed))
        else:
            state_ref[0, c] = jnp.zeros((DK, DV), BF)
            right = twice(beta) * vc
        fresh = dot_nn(found[c], right.astype(BF)).astype(BF)
        fresh_ref[c * CHUNK : (c + 1) * CHUNK, :] = fresh
        out = dot_nn(attend[c], fresh)
        if c:
            out = out + twice(reach) * dot_nn(qc, packed)
        if c < chunks - 1:
            grown = dot_tn((ends * kc.astype(F32)).astype(BF), fresh)
            state = grown + twice(reach[CHUNK - 1 : CHUNK]) * state if c else grown
        out_ref[c * CHUNK : (c + 1) * CHUNK, :] = out
        unit = out * lax.rsqrt(jnp.mean(out * out, axis=-1, keepdims=True) + out_floor)
        gate = gate_ref[c * CHUNK : (c + 1) * CHUNK, :].astype(F32)
        mixed_ref[c * CHUNK : (c + 1) * CHUNK, :] = (unit * gain_ref[...] * (gate * sigmoid(gate))).astype(BF)


def whole(shape):
    return pl.BlockSpec(shape, lambda h: (0,) * len(shape))


def per_head(rows):
    return pl.BlockSpec((1, 1, rows), lambda h: (h, 0, 0))


def columns(rows, width, at):
    return pl.BlockSpec((rows, width), lambda h: (0, at + h))


def mixer(projected, at, seg, segrow, gamma, beta, taps, gain):
    rows, held = projected.shape[0], projected.shape[1] // (2 * DK + 2 * DV)
    chunks, heads = rows // CHUNK, gamma.shape[0]
    return pl.pallas_call(
        mix_kernel,
        grid=(heads,),
        in_specs=[
            columns(rows, DK, at), columns(rows, DK, held + at), columns(rows, DV, held + at), columns(rows, DV, 2 * held + at),
            whole((rows, CHUNK)), whole((8, rows)), whole((heads, rows)), per_head(rows),
            columns(CONV, DK, at), columns(CONV, DK, held + at), columns(CONV, DV, held + at),
            whole((1, DV)),
        ],
        out_specs=[
            columns(rows, DV, 0), columns(rows, DV, 0), columns(rows, DV, 0),
            pl.BlockSpec((1, chunks, CHUNK, CHUNK), lambda h: (h, 0, 0, 0)),
            pl.BlockSpec((1, chunks, DK, DV), lambda h: (h, 0, 0, 0)),
        ],
        out_shape=[
            jax.ShapeDtypeStruct((rows, heads * DV), BF),
            jax.ShapeDtypeStruct((rows, heads * DV), F32),
            jax.ShapeDtypeStruct((rows, heads * DV), BF),
            jax.ShapeDtypeStruct((heads, chunks, CHUNK, CHUNK), BF),
            jax.ShapeDtypeStruct((heads, chunks, DK, DV), BF),
        ],
        scratch_shapes=[pltpu.VMEM((CONV - 1, rows, CHUNK), F32), pltpu.VMEM((heads, 1, rows), F32)],
        compiler_params=pltpu.CompilerParams(vmem_limit_bytes=32 * 2**20),
        cost_estimate=pl.CostEstimate(flops=heads * int(5e9), bytes_accessed=heads * int(4e6), transcendentals=0),
    )(projected, projected, projected, projected, seg, segrow, gamma, beta[:, None], taps, taps, taps, gain)


def back_kernel(
    q_ref, k_ref, v_ref, gate_ref, seg_ref, segrow_ref, gamma_ref, beta_ref,
    tapq_ref, tapk_ref, tapv_ref, gain_ref, out_ref, fresh_ref, inv_ref, state_ref, back_ref,
    dq_ref, dk_ref, dv_ref, dgate_ref, dtapq_ref, dtapk_ref, dtapv_ref, dgain_ref, dgamma_ref, dbeta_ref,
    mask_ref, sums_ref, lift_ref,
):
    h = pl.program_id(0)

    @pl.when(h == 0)
    def _():
        fill_masks(seg_ref, mask_ref)
        fill_sums(gamma_ref, sums_ref)
        dgain_ref[...] = jnp.zeros_like(dgain_ref)

    rows = q_ref.shape[0]
    chunks = rows // CHUNK

    def active(ref, tap_ref):
        total = convolve(ref[...].astype(F32), tap_ref[...], mask_ref)
        s = sigmoid(total)
        return total * s, s * (1.0 + total * (1.0 - s))

    qf, qslope = active(q_ref, tapq_ref)
    kraw, kslope = active(k_ref, tapk_ref)
    vf, vslope = active(v_ref, tapv_ref)
    kscale = lax.rsqrt(jnp.sum(kraw * kraw, axis=-1, keepdims=True) + epsilon)
    kunit = kraw * kscale
    q, k, v = qf.astype(BF), kunit.astype(BF), vf.astype(BF)
    cut = lambda x, c: x[c * CHUNK : (c + 1) * CHUNK]
    gain = gain_ref[...]
    carried = None
    dqs, dks, dvs = [None] * chunks, [None] * chunks, [None] * chunks
    dgain = jnp.zeros((1, DV), F32)
    for c in reversed(range(chunks)):
        span = pl.ds(c * CHUNK, CHUNK)
        beta, decays, strict, ends, reach = chunk_scales(c, h, sums_ref, beta_ref, seg_ref, segrow_ref)
        kc, qc, vc = cut(k, c), cut(q, c), cut(v, c).astype(F32)
        kcf, qcf = kc.astype(F32), qc.astype(F32)
        out, gate, back = out_ref[span, :], gate_ref[span, :].astype(F32), back_ref[span, :].astype(F32)
        p = lax.rsqrt(jnp.mean(out * out, axis=-1, keepdims=True) + out_floor)
        z = out * p
        s = sigmoid(gate)
        a = back * (gate * s)
        az = a * z
        dgain = dgain + jnp.sum(az, axis=0, keepdims=True)
        dgate_ref[span, :] = (back * (z * gain) * (s * (1.0 + gate * (1.0 - s)))).astype(BF)
        dout = p * (a * gain - z * jnp.mean(az * gain, axis=-1, keepdims=True))
        doutb = dout.astype(BF)
        key_key = dot_nt(kc, kc)
        query_key = dot_nt(qc, kc)
        attend = (decays * query_key).astype(BF)
        fresh = fresh_ref[span, :]
        found = inv_ref[0, c]
        dfresh = dot_tn(attend, doutb)
        if carried is not None:
            carriedb = carried.astype(BF)
            dfresh = dfresh + twice(ends) * dot_nn(kc, carriedb)
        dscore = decays * dot_nt(doutb, fresh)
        dright = dot_tn(found, dfresh.astype(BF))
        drightb = dright.astype(BF)
        dsystem = dot_nt(drightb, fresh)
        dvs[c] = twice(beta) * dright
        m = key_key * (strict * dsystem)
        dkk = (beta * strict) * dsystem
        tally = query_key * dscore - beta * m
        dscoreb = dscore.astype(BF)
        dq = dot_nn(dscoreb, kc)
        dk = dot_tn(dscoreb, qc) - dot_nn((dkk + dkk.T).astype(BF), kc)
        side = tally
        edge = None
        if carried is not None:
            dkf = dot_nt((twice(ends) * fresh.astype(F32)).astype(BF), carriedb)
            dk = dk + dkf
            moved = kcf * dkf
            side = side - moved
            edge = jnp.sum(moved, axis=0, keepdims=True)
        if c:
            state = state_ref[0, c]
            rout = (twice(reach) * dout).astype(BF)
            given = dot_nn(kc, state)
            drest = dright * (vc - twice(reach) * given)
            w = (-twice(beta * reach) * dright).astype(BF)
            dqs1 = dot_nt(rout, state)
            dks1 = dot_nt(w, state)
            dq = dq + dqs1
            dk = dk + dks1
            side = side + qcf * dqs1 + kcf * dks1
            grown = dot_tn(jnp.concatenate([qc, kc], axis=0), jnp.concatenate([rout, w], axis=0))
            if carried is not None:
                last = reach[CHUNK - 1 : CHUNK]
                kept = carried * state.astype(F32)
                edge = edge + last * jnp.sum(kept[:, :CHUNK] + kept[:, CHUNK:], axis=0, keepdims=True)
                carried = twice(last) * carried + grown
            else:
                carried = grown
        else:
            drest = dright * vc
        dqs[c] = dq
        dks[c] = dk
        dbeta = drest[:, :CHUNK] + drest[:, CHUNK:] - m
        dbeta_ref[0, :, span] = jnp.sum(dbeta.T, axis=0, keepdims=True)
        lift = jnp.sum(side.T - tally, axis=0, keepdims=True)
        if edge is not None:
            lane = lax.broadcasted_iota(jnp.int32, (1, CHUNK), 1)
            lift = lift + jnp.where(lane == CHUNK - 1, jnp.sum(edge, axis=1, keepdims=True), 0.0)
        lift_ref[h, :, span] = lift
    dgain_ref[...] += dgain

    def spread(grad, ref, tap_ref, to_ref, dtap_ref):
        x, taps = ref[...].astype(F32), tap_ref[...]
        total = grad * taps[0:1]
        sums = [jnp.sum(grad * x, axis=0, keepdims=True)]
        for shift in range(1, CONV):
            masked = grad * wide(mask_ref[shift - 1], x.shape[1])
            sums.append(jnp.sum(masked * pltpu.roll(x, shift, 0), axis=0, keepdims=True))
            total = total + pltpu.roll(masked, rows - shift, 0) * taps[shift : shift + 1]
        to_ref[...] = total.astype(BF)
        dtap_ref[...] = jnp.concatenate(sums, axis=0)

    spread(jnp.concatenate(dqs, axis=0) * qslope, q_ref, tapq_ref, dq_ref, dtapq_ref)
    dk = jnp.concatenate(dks, axis=0)
    dk = kscale * (dk - kunit * jnp.sum(kunit * dk, axis=-1, keepdims=True))
    spread(dk * kslope, k_ref, tapk_ref, dk_ref, dtapk_ref)
    spread(jnp.concatenate(dvs, axis=0) * vslope, v_ref, tapv_ref, dv_ref, dtapv_ref)

    @pl.when(h == pl.num_programs(0) - 1)
    def _():
        heads = gamma_ref.shape[0]
        lane = lax.broadcasted_iota(jnp.int32, (heads, CHUNK), 1)
        for c in range(chunks):
            span = pl.ds(c * CHUNK, CHUNK)
            total = jnp.concatenate([lift_ref[i, :, span] for i in range(heads)], axis=0)
            step = 1
            while step < CHUNK:
                total = total + jnp.where(lane < CHUNK - step, pltpu.roll(total, CHUNK - step, 1), 0.0)
                step *= 2
            dgamma_ref[:, span] = total


def mixer_back(projected, at, seg, segrow, gamma, beta, taps, gain, out, fresh, inv, state, back, back_at):
    rows, held = projected.shape[0], projected.shape[1] // (2 * DK + 2 * DV)
    chunks, heads = rows // CHUNK, gamma.shape[0]
    return pl.pallas_call(
        back_kernel,
        grid=(heads,),
        in_specs=[
            columns(rows, DK, at), columns(rows, DK, held + at), columns(rows, DV, held + at), columns(rows, DV, 2 * held + at),
            whole((rows, CHUNK)), whole((8, rows)), whole((heads, rows)), per_head(rows),
            columns(CONV, DK, at), columns(CONV, DK, held + at), columns(CONV, DV, held + at),
            whole((1, DV)),
            columns(rows, DV, 0), columns(rows, DV, 0),
            pl.BlockSpec((1, chunks, CHUNK, CHUNK), lambda h: (h, 0, 0, 0)),
            pl.BlockSpec((1, chunks, DK, DV), lambda h: (h, 0, 0, 0)),
            columns(rows, DV, back_at),
        ],
        out_specs=[
            columns(rows, DK, 0), columns(rows, DK, 0), columns(rows, DV, 0), columns(rows, DV, 0),
            columns(CONV, DK, 0), columns(CONV, DK, 0), columns(CONV, DV, 0),
            whole((1, DV)), whole((heads, rows)), per_head(rows),
        ],
        out_shape=[
            jax.ShapeDtypeStruct((rows, heads * DK), BF),
            jax.ShapeDtypeStruct((rows, heads * DK), BF),
            jax.ShapeDtypeStruct((rows, heads * DV), BF),
            jax.ShapeDtypeStruct((rows, heads * DV), BF),
            jax.ShapeDtypeStruct((CONV, heads * DK), F32),
            jax.ShapeDtypeStruct((CONV, heads * DK), F32),
            jax.ShapeDtypeStruct((CONV, heads * DV), F32),
            jax.ShapeDtypeStruct((1, DV), F32),
            jax.ShapeDtypeStruct((heads, rows), F32),
            jax.ShapeDtypeStruct((heads, 1, rows), F32),
        ],
        scratch_shapes=[
            pltpu.VMEM((CONV - 1, rows, CHUNK), F32),
            pltpu.VMEM((heads, 1, rows), F32),
            pltpu.VMEM((heads, 1, rows), F32),
        ],
        compiler_params=pltpu.CompilerParams(vmem_limit_bytes=32 * 2**20),
        cost_estimate=pl.CostEstimate(flops=heads * int(6e9), bytes_accessed=heads * int(5e6), transcendentals=0),
    )(projected, projected, projected, projected, seg, segrow, gamma, beta[:, None], taps, taps, taps, gain, out, fresh, inv, state, back)


TILE = 256


def ffn_in_kernel(x_ref, gate_w_ref, up_w_ref, gate_ref, up_ref, inner_ref):
    gate, up = dot_nn(x_ref[...], gate_w_ref[...]), dot_nn(x_ref[...], up_w_ref[...])
    gate_ref[...] = gate.astype(BF)
    up_ref[...] = up.astype(BF)
    inner_ref[...] = (gate * sigmoid(gate) * up).astype(BF)


def ffn_in(x, weight):
    rows, depth = x.shape
    width = weight.shape[1] // 2
    tiles = width // TILE
    return pl.pallas_call(
        ffn_in_kernel,
        grid=(tiles,),
        in_specs=[whole((rows, depth)), columns(depth, TILE, 0), columns(depth, TILE, tiles)],
        out_specs=[columns(rows, TILE, 0)] * 3,
        out_shape=[jax.ShapeDtypeStruct((rows, width), BF)] * 3,
        compiler_params=pltpu.CompilerParams(vmem_limit_bytes=32 * 2**20),
        cost_estimate=pl.CostEstimate(flops=4 * rows * depth * width, bytes_accessed=4 * depth * width, transcendentals=0),
    )(x, weight, weight)


def ffn_out_kernel(c_ref, gate_ref, up_ref, inner_ref, down_w_ref, gate_w_ref, up_w_ref, back_ref, down_ref, x_back_ref):
    @pl.when(pl.program_id(0) == 0)
    def _():
        down_ref[...] = jnp.zeros_like(down_ref)
        x_back_ref[...] = jnp.zeros_like(x_back_ref)

    inner_back = dot_nt(c_ref[...], down_w_ref[...])
    gate, up = gate_ref[...].astype(F32), up_ref[...].astype(F32)
    s = sigmoid(gate)
    gate_back = (inner_back * up * (s * (1.0 + gate * (1.0 - s)))).astype(BF)
    up_back = (inner_back * (gate * s)).astype(BF)
    back_ref[0] = gate_back
    back_ref[1] = up_back
    down_ref[...] += dot_nn(inner_ref[...], down_w_ref[...])
    x_back_ref[...] += dot_nt(gate_back, gate_w_ref[...]) + dot_nt(up_back, up_w_ref[...])


def ffn_out(cotangent, gate, up, inner, down_w, gate_up_w):
    rows, width = gate.shape
    depth = cotangent.shape[1]
    tiles = width // TILE
    return pl.pallas_call(
        ffn_out_kernel,
        grid=(tiles,),
        in_specs=[
            whole((rows, depth)),
            columns(rows, TILE, 0), columns(rows, TILE, 0), columns(rows, TILE, 0),
            pl.BlockSpec((TILE, depth), lambda h: (h, 0)),
            columns(depth, TILE, 0), columns(depth, TILE, tiles),
        ],
        out_specs=[pl.BlockSpec((2, rows, TILE), lambda h: (0, 0, h)), whole((rows, depth)), whole((rows, depth))],
        out_shape=[
            jax.ShapeDtypeStruct((2, rows, width), BF),
            jax.ShapeDtypeStruct((rows, depth), F32),
            jax.ShapeDtypeStruct((rows, depth), F32),
        ],
        compiler_params=pltpu.CompilerParams(vmem_limit_bytes=32 * 2**20),
        cost_estimate=pl.CostEstimate(flops=8 * rows * depth * width, bytes_accessed=6 * depth * width, transcendentals=0),
    )(cotangent, gate, up, inner, down_w, gate_up_w, gate_up_w)


SHIFTS = (1, 2, 3)


def place():
    rep = lax.axis_index("rep")
    core, x, y = rep % 2, (rep // 2) % 2, (rep // 4) % 2
    a = jnp.where(core == 0, x, y)
    b = jnp.where(core == 0, y, x)
    return core, a, b


def hop(value, kind):
    count = lax.axis_size("rep")
    if kind == "core":
        pairs = [(i, i ^ 1) for i in range(count)]
    elif kind == "first":
        pairs = [(i, i ^ (4 if i & 1 else 2)) for i in range(count)]
    elif kind == "second":
        pairs = [(i, i ^ (2 if i & 1 else 4)) for i in range(count)]
    else:
        pairs = [(i, i ^ kind) for i in range(count)]
    return lax.ppermute(value, "rep", pairs)


def shift(value, by):
    count = lax.axis_size("shard")
    return lax.ppermute(value, "shard", [(i, (i + by) % count) for i in range(count)])


def after(value, *others):
    if not others:
        return value
    return lax.optimization_barrier((value,) + others)[0]


def assemble_kernel(along, size, rows, at_ref, own_ref, *refs):
    pieces, whole_ref = refs[:-1], refs[-1]
    whole_ref[pl.ds(pl.multiple_of(at_ref[0] * rows, 16), rows), :] = own_ref[...]
    n = 1
    for piece in pieces:
        for slot in range(piece.shape[0]):
            block, part = at_ref[n], at_ref[n + 1]
            n += 2
            if along == 0:
                whole_ref[pl.ds(pl.multiple_of(block * rows + part * size, 16), size), :] = piece[slot]
            else:
                whole_ref[pl.ds(pl.multiple_of(block * rows, 16), rows), pl.ds(pl.multiple_of(part * size, 128), size)] = piece[slot]


class Gather:
    def __init__(self, weight, along):
        self.weight, self.along = weight, along
        self.size = weight.shape[along] // 8

    def deep(self, *tokens):
        core, a, b = place()
        mine = lax.dynamic_slice_in_dim(self.weight, (core * 4 + a * 2 + b) * self.size, self.size, self.along)
        mine = after(mine, *tokens)
        self.raw = [shift(mine, by) for by in range(1, lax.axis_size("shard"))]

    def first(self, *tokens):
        count = len(self.raw)
        raw = lax.optimization_barrier(tuple(self.raw) + tokens)[:count]
        self.here = jnp.stack(raw)
        self.come = hop(self.here, "first")

    def second(self, *tokens):
        self.pair = jnp.concatenate([self.here, after(self.come, *tokens)])
        self.others = hop(self.pair, "second")
        self.pair_core = hop(self.pair, "core")

    def core(self, *tokens):
        self.others_in = after(self.others, *tokens)
        self.others_core = hop(self.others_in, "core")

    def full(self, *tokens):
        core, a, b = place()
        z, count = lax.axis_index("shard"), lax.axis_size("shard")
        part, other = core * 4 + a * 2 + b, (1 - core) * 4 + b * 2 + a
        blocks = [(z - by) % count for by in range(1, count)]
        at = [z]
        for home, flips in ((part, (0, 2)), (part, (1, 3)), (other, (0, 2)), (other, (1, 3))):
            for flip in flips:
                for block in blocks:
                    at += [block, home ^ flip]
        rows, width = self.weight.shape
        pieces = [self.pair, self.others_in, self.pair_core, after(self.others_core, *tokens)]
        return pl.pallas_call(
            functools.partial(assemble_kernel, self.along, self.size, rows),
            in_specs=[pl.BlockSpec(memory_space=pltpu.SMEM)] + [pl.BlockSpec(memory_space=pltpu.VMEM)] * 5,
            out_specs=pl.BlockSpec(memory_space=pltpu.VMEM),
            compiler_params=pltpu.CompilerParams(vmem_limit_bytes=48 * 2**20),
            out_shape=jax.ShapeDtypeStruct((rows * count, width), BF),
        )(jnp.stack(at).astype(jnp.int32), self.weight, *pieces)


def pick(value, at, size, axis):
    return lax.dynamic_slice_in_dim(value, at * size, size, axis)


def join(bit, mine, theirs, axis):
    return jnp.where(bit == 0, jnp.concatenate([mine, theirs], axis), jnp.concatenate([theirs, mine], axis))


class Total:
    def __init__(self, left, right):
        self.left, self.right = left, right
        self.count = lax.axis_size("shard")
        self.rows = left.shape[1] // self.count
        self.quarter = right.size // right.shape[-2] // 4

    def core(self, *tokens):
        core, a, b = place()
        half = 2 * self.quarter
        right = after(self.right, *tokens) if tokens else self.right
        if right.ndim == 3:
            self.own, other = (pick(right, n, 1, 0)[0] for n in (core, 1 - core))
        else:
            self.own, other = (pick(right, n, half, 1) for n in (core, 1 - core))
        self.given = dot_tn(self.left, other).astype(BF)
        self.got = hop(self.given, "core")
        return self.got

    def first(self, *tokens):
        core, a, b = place()
        self.got = after(self.got, *tokens)
        sent = dot_tn(self.left, pick(self.own, 1 - a, self.quarter, 1)) + pick(self.got, 1 - a, self.quarter, 1).astype(F32)
        self.sent = sent.astype(BF)
        self.got_first = hop(self.sent, "first")

    def second(self, *tokens):
        core, a, b = place()
        got_first = after(self.got_first, *tokens)
        kept = dot_tn(self.left, pick(self.own, a, self.quarter, 1)) + pick(self.got, a, self.quarter, 1).astype(F32)
        kept = (kept + got_first.astype(F32)).astype(BF).reshape(self.count, self.rows, self.quarter)
        self.axis = 2 if self.quarter % 256 == 0 else 1
        size = kept.shape[self.axis] // 2
        self.passed = pick(kept, 1 - b, size, self.axis)
        self.mine = pick(kept, b, size, self.axis)
        self.got_second = hop(self.passed, "second")

    def deep(self, *tokens):
        z = lax.axis_index("shard")
        kept = (self.mine.astype(F32) + after(self.got_second, *tokens).astype(F32)).astype(BF)
        extra = 8
        while extra < lax.axis_size("rep"):
            kept = (kept.astype(F32) + hop(kept, extra).astype(F32)).astype(BF)
            extra *= 2
        self.kept = kept
        self.raw = [shift(pick(kept, (z + by) % self.count, 1, 0)[0], by) for by in range(1, self.count)]

    def finish(self, *tokens):
        total = pick(self.kept, lax.axis_index("shard"), 1, 0)[0].astype(F32)
        for piece in lax.optimization_barrier(tuple(self.raw) + tokens)[: len(self.raw)]:
            total = total + piece.astype(F32)
        self.done = total.astype(BF)


def final_kernel(copies, at_ref, *refs):
    pieces, outs = refs[:8], refs[8:]
    n = 0
    for piece in pieces:
        for start, size, width, out, moving, fixed in copies:
            block = piece[start : start + size, :width].astype(F32)
            if moving == "both":
                rows = pl.ds(pl.multiple_of(at_ref[n] * size, 8), size)
                outs[out][rows, pl.ds(pl.multiple_of(at_ref[n + 1] * 128, 128), width)] = block
                n += 2
            else:
                outs[out][:, pl.ds(pl.multiple_of(at_ref[n] * 128, 128), width)] = block
                n += 1


class Spread:
    def __init__(self, done):
        self.done = done
        self.theirs = hop(done, "second")

    def first(self, *tokens):
        self.pair = jnp.stack([self.done, after(self.theirs, *tokens)])
        self.others = hop(self.pair, "first")

    def core(self, *tokens):
        self.four = jnp.concatenate([self.pair, after(self.others, *tokens)])
        self.over = hop(self.four, "core")

    def parts(self, *tokens):
        over = after(self.over, *tokens)
        return [self.four[n] for n in range(4)] + [over[n] for n in range(4)]


def part_numbers():
    core, a, b = place()
    home, away = core * 4 + a * 2 + b, (1 - core) * 4 + b * 2 + a
    return [home ^ n for n in range(4)] + [away ^ n for n in range(4)]


def finish_totals(pieces, copies, at, shapes):
    return pl.pallas_call(
        functools.partial(final_kernel, copies),
        in_specs=[pl.BlockSpec(memory_space=pltpu.SMEM)] + [pl.BlockSpec(memory_space=pltpu.VMEM)] * 8,
        out_specs=[pl.BlockSpec(memory_space=pltpu.VMEM)] * len(shapes),
        compiler_params=pltpu.CompilerParams(vmem_limit_bytes=48 * 2**20),
        out_shape=[jax.ShapeDtypeStruct(s, F32) for s in shapes],
    )(jnp.stack(at).astype(jnp.int32), *pieces)


def rms_scale(values, gain):
    return values * lax.rsqrt(jnp.mean(values * values, axis=-1, keepdims=True) + epsilon) * gain


def as_rows(x, count):
    flat = x.astype(F32).reshape(count, -1)
    return jnp.pad(flat, ((0, 0), (0, -flat.shape[1] % 1024))).reshape(count, -1, 128)


def from_rows(rows, shapes):
    found, start = [], 0
    for shape in shapes:
        size = math.prod(shape)
        deep = -(-size // 1024) * 8
        piece = rows[:, start : start + deep].reshape(rows.shape[0], -1)[:, :size]
        found.append(piece.reshape((rows.shape[0],) + shape))
        start += deep
    return found


def share_small(arrays):
    count = lax.axis_size("shard")
    z = lax.axis_index("shard")
    flat = jnp.concatenate([as_rows(x, 1) for x in arrays], axis=1)
    every = jnp.zeros((count,) + flat.shape[1:], F32)
    every = lax.dynamic_update_slice_in_dim(every, flat, z, 0)
    for by in range(1, count):
        every = lax.dynamic_update_slice_in_dim(every, shift(flat, by), (z - by) % count, 0)
    return from_rows(every, [x.shape for x in arrays])


class Small:
    def __init__(self, arrays):
        self.shapes = [x.shape[1:] for x in arrays]
        count, z = lax.axis_size("shard"), lax.axis_index("shard")
        flat = jnp.concatenate([as_rows(x, count) for x in arrays], axis=1)
        self.total = pick(flat, z, 1, 0)
        self.raw = [shift(pick(flat, (z + by) % count, 1, 0), by) for by in range(1, count)]
        self.step = 1

    def add(self, *tokens):
        for piece in lax.optimization_barrier(tuple(self.raw) + tokens)[: len(self.raw)]:
            self.total = self.total + piece
        if self.step < lax.axis_size("rep"):
            self.raw = [hop(self.total, self.step)]
            self.step *= 2
        else:
            self.raw = []

    def finish(self):
        while self.raw:
            self.add()
        return [x[0] for x in from_rows(self.total, self.shapes)]


def beside(blocks):
    return jnp.concatenate(list(blocks), axis=-1)


def parted(x):
    count = lax.axis_size("shard")
    return jnp.moveaxis(x.reshape(x.shape[:-1] + (count, -1)), -2, 0)


GROUPS = 2
STEPS = 4


def group_columns(x, g):
    wide, deep = KEYS // GROUPS, VALS // GROUPS
    cuts = [x[:, n * KEYS + g * wide : n * KEYS + (g + 1) * wide] for n in (0, 1)]
    start = 2 * KEYS
    while start < x.shape[1]:
        cuts.append(x[:, start + g * deep : start + (g + 1) * deep])
        start += VALS
    return jnp.concatenate(cuts, axis=1)


def mix_final_kernel(blocks, at_ref, *refs):
    for n, piece in enumerate(refs[:-1]):
        for m in range(blocks):
            to = pl.ds(pl.multiple_of(at_ref[n * blocks + m] * 128, 128), 128)
            refs[-1][:, to] = piece[:, m * 128 : (m + 1) * 128].astype(F32)


def finish_mix(pieces, blocks, at, shape):
    return pl.pallas_call(
        functools.partial(mix_final_kernel, blocks),
        in_specs=[pl.BlockSpec(memory_space=pltpu.SMEM)] + [pl.BlockSpec(memory_space=pltpu.VMEM)] * len(pieces),
        out_specs=pl.BlockSpec(memory_space=pltpu.VMEM),
        compiler_params=pltpu.CompilerParams(vmem_limit_bytes=48 * 2**20),
        out_shape=jax.ShapeDtypeStruct(shape, F32),
    )(jnp.stack(at).astype(jnp.int32), *pieces)


def body(
    hidden_in,
    segment_ids,
    norm_gains,
    w_mix_in,
    w_decay,
    decay_params,
    conv_weight,
    out_gain,
    w_mix_out,
    w_gate_up,
    w_down,
    cotangent,
):
    rows = hidden_in.shape[0]
    small = share_small([norm_gains, decay_params, conv_weight, out_gain[None], w_decay])
    gains, rates, taps, gain_row = (beside(x) for x in small[:4])
    decay_full = small[4].reshape(-1, 2 * HEADS).astype(BF)

    ga, gb = (Gather(group_columns(w_mix_in, g), 1) for g in range(GROUPS))
    go, gu, gd = Gather(w_mix_out, 1), Gather(w_gate_up, 0), Gather(w_down, 1)
    ga.deep()
    ga.first()
    ga.second()
    ga.core()
    gb.deep(ga.others)

    hidden = hidden_in.astype(F32)
    normed_one_f, norm_one_pull = jax.vjp(rms_scale, hidden, gains[0])
    normed_one = normed_one_f.astype(BF)
    logits = dot_nt(decay_full.T, normed_one)
    rate, bias = jnp.exp(rates[0])[:, None], rates[1][:, None]
    gamma = -rate * jax.nn.softplus(logits[:HEADS] + bias)
    beta = jax.nn.sigmoid(logits[HEADS:])
    seg = jnp.broadcast_to(segment_ids[:, None], (rows, CHUNK))
    segrow = jnp.broadcast_to(segment_ids[None], (8, rows))
    tap_groups = [group_columns(taps, g) for g in range(GROUPS)]
    heads = HEADS // STEPS

    mix_in = [ga.full(), None]
    gb.first(mix_in[0])
    projected = [dot_nn(normed_one, mix_in[0]), None]
    gb.second(projected[0])
    go.deep(projected[0], *gb.raw)
    kept = []

    def mix(n, *tokens):
        g, at = n * GROUPS // STEPS, n % (STEPS // GROUPS) * heads
        span = slice(n * heads, (n + 1) * heads)
        gate = after(gamma[span], *tokens) if tokens else gamma[span]
        kept.append(mixer(projected[g], at, seg, segrow, gate, beta[span], tap_groups[g], gain_row))
        return kept[-1][0]

    done = mix(0)
    gb.core(done)
    gu.deep(done, *go.raw)
    done = mix(1)
    mix_in[1] = gb.full(done)
    go.first(done)
    projected[1] = dot_nn(after(normed_one, done), mix_in[1])
    go.second(projected[1])
    gu.first(projected[1])
    gd.deep(projected[1], *gu.raw)
    done = mix(2, gu.here, go.pair)
    gu.second(done)
    go.core(done)
    done = mix(3, gu.pair, *gd.raw)
    gd.first(done)
    mix_out = go.full()
    mixed_out = jnp.concatenate([x[0] for x in kept], axis=1)
    residual = hidden + dot_nn(mixed_out, mix_out)
    normed_two_f, norm_two_pull = jax.vjp(rms_scale, residual, gains[1])
    normed_two = normed_two_f.astype(BF)
    gu.core(normed_two)
    gate_up_full = gu.full()
    gd.second(gate_up_full)
    gate, up, inner = ffn_in(after(normed_two, gd.pair), gate_up_full)
    gd.core(inner)
    down_full = gd.full()
    t_down = Total(inner, cotangent)
    t_down.core()
    gate_up_back, down, normed_two_back = ffn_out(
        after(cotangent, t_down.given), gate, up, inner, down_full, gate_up_full
    )
    t_gu = Total(normed_two, gate_up_back)
    t_gu.core()
    t_down.first(t_gu.given)
    result = (residual + down).astype(BF)
    residual_part, gain_two = norm_two_pull(after(normed_two_back, t_down.sent))
    t_gu.first(gain_two)
    residual_back = cotangent.astype(F32) + residual_part
    branch_back = after(residual_back.astype(BF), t_gu.sent)
    t_out = Total(mixed_out, branch_back)
    t_out.core()
    mixed_back = dot_nt(branch_back, mix_out)

    backs = []

    def mix_back(n, *tokens):
        g, at = n * GROUPS // STEPS, n % (STEPS // GROUPS) * heads
        span = slice(n * heads, (n + 1) * heads)
        gate = after(gamma[span], *tokens)
        backs.append(
            mixer_back(projected[g], at, seg, segrow, gate, beta[span], tap_groups[g], gain_row, *kept[n][1:], mixed_back, n * heads)
        )
        return backs[-1][0]

    def group_back(g):
        each = STEPS // GROUPS
        return jnp.concatenate([x[n] for n in range(4) for x in backs[g * each : (g + 1) * each]], axis=1)

    done = mix_back(0, t_gu.sent, t_out.given)
    t_out.first(done)
    t_down.second(done)
    done = mix_back(1, t_out.sent, t_down.passed)
    back_a = group_back(0)
    t_a = Total(normed_one, back_a)
    t_a.core(done)
    t_down.deep(done)
    done = mix_back(2, t_a.given, t_down.kept)
    t_gu.second(done)
    t_a.first(t_gu.passed)
    t_out.second(t_a.sent)
    done = mix_back(3, t_a.sent, t_out.passed)
    t_down.finish(done)
    t_gu.deep(done)
    back_b = group_back(1)
    t_b = Total(normed_one, back_b)
    t_b.core(t_gu.kept)
    t_out.deep(t_b.given)
    dgain = sum(x[7] for x in backs)
    dgamma = jnp.concatenate([x[8] for x in backs], axis=0)
    dbeta = jnp.concatenate([x[9][:, 0] for x in backs], axis=0)
    slope = -dgamma * rate * jax.nn.sigmoid(logits[:HEADS] + bias)
    logits_back = jnp.concatenate([slope, dbeta * beta * (1.0 - beta)], axis=0).astype(BF)
    grad_rates = jnp.stack([jnp.sum(dgamma * gamma, axis=1), jnp.sum(slope, axis=1)])
    grad_taps = jnp.concatenate([x[n] for n in (4, 5, 6) for x in backs], axis=1)
    grad_decay = lax.dot_general(normed_one, logits_back, (((0,), (1,)), ((), ())), preferred_element_type=F32)
    near = dot_nt(after(back_a, t_b.given), mix_in[0]) + lax.dot_general(
        logits_back, decay_full, (((0,), (1,)), ((), ())), preferred_element_type=F32
    )
    t_b.first(near)
    near = near + dot_nt(after(back_b, t_b.sent), mix_in[1])
    t_a.second(t_b.sent)
    hidden_part, gain_one = norm_one_pull(after(near, t_a.passed))
    grad_in = residual_back + hidden_part
    t_b.second(gain_one)
    t_a.deep(t_b.passed)
    t_gu.finish(t_b.passed)
    t_out.finish(t_b.passed)
    count = lax.axis_size("shard")
    small_total = Small([
        parted(jnp.stack([gain_one, gain_two])),
        grad_decay.reshape(count, -1, 2 * HEADS),
        parted(grad_rates),
        parted(grad_taps),
        parted(dgain[0]),
    ])
    numbers = part_numbers()
    wide = t_gu.done.shape[1] // 128
    merged = jnp.concatenate(
        [t_down.done, t_out.done] + [t_gu.done[:, n * 128 : (n + 1) * 128] for n in range(wide)]
    )
    s_rest = Spread(merged)
    t_b.deep(s_rest.done)
    small_total.add(t_b.kept)
    s_rest.first(t_b.kept)
    t_a.finish(s_rest.pair)
    t_b.finish(s_rest.pair)
    s_mix = Spread(jnp.concatenate([t_a.done, t_b.done], axis=1))
    small_total.add(s_mix.done)
    s_rest.core(s_mix.done)
    s_mix.first(s_rest.four)
    small_total.add(s_mix.pair)
    copies, at, start = [], [], 0
    for out, deep in enumerate((t_down.rows, t_out.rows)):
        copies.append((start, deep, 128, out, "columns", 0))
        start += deep
    for n in range(wide):
        copies.append((start, t_gu.rows // 2, 128, 2, "both", n))
        start += t_gu.rows // 2
    for part in numbers:
        at += [part, part]
        for n in range(wide):
            at += [part % 2, part // 2 * wide + n]
    grad_down, grad_mix_out, grad_gate_up = finish_totals(
        s_rest.parts(s_mix.pair), copies, at, [w_down.shape, w_mix_out.shape, w_gate_up.shape]
    )
    s_mix.core(grad_down)
    small_total.add(s_mix.four)
    parts = small_total.finish()
    each = t_a.done.shape[1] // 128
    copies, at = [], []
    edge, wide, tall = 0, KEYS // GROUPS // 128, VALS // GROUPS // 128
    for part in numbers:
        for g in range(GROUPS):
            for n in range(each):
                block = part * each + n
                to = block + g * wide
                to = jnp.where(block >= wide, block - wide + KEYS // 128 + g * wide, to)
                to = jnp.where(block >= 2 * wide, block - 2 * wide + 2 * KEYS // 128 + g * tall, to)
                to = jnp.where(block >= 2 * wide + tall, block - 2 * wide - tall + (2 * KEYS + VALS) // 128 + g * tall, to)
                at.append(to)
    pieces = s_mix.parts()
    grad_mix_in = finish_mix(pieces, GROUPS * each, at, w_mix_in.shape)
    return (
        result,
        grad_in,
        parts[0],
        grad_mix_in,
        parts[1],
        parts[2],
        parts[3],
        parts[4],
        grad_mix_out,
        grad_gate_up,
        grad_down,
    )


def solution(mesh):
    rows, columns_, both = P("shard", None), P(None, "shard"), P(("rep", "shard"), None)
    return jax.shard_map(
        body,
        mesh=mesh,
        in_specs=(both, P(("rep", "shard")), columns_, rows, rows, columns_, columns_, P("shard"), rows, rows, rows, both),
        out_specs=(both, both, columns_, rows, rows, columns_, columns_, P("shard"), rows, rows, rows),
        check_vma=False,
    )
```

```python
import functools
import math

import jax
import jax.numpy as jnp
from jax import lax
from jax.experimental import pallas as pl
from jax.experimental.pallas import tpu as pltpu
from jax.sharding import PartitionSpec as P

HEADS = 8
DK = 128
DV = 256
FF = 2816
CONV = 4
KEYS = 1024
VALS = 2048
CHUNK = 128
epsilon = 1e-06
out_floor = 0.01
BF = jnp.bfloat16
F32 = jnp.float32


def dot_nn(a, b):
    return jnp.dot(a, b, preferred_element_type=F32)


def dot_nt(a, b):
    return lax.dot_general(a, b, (((1,), (1,)), ((), ())), preferred_element_type=F32)


def dot_tn(a, b):
    return lax.dot_general(a, b, (((0,), (0,)), ((), ())), preferred_element_type=F32)


def twice(x):
    return jnp.concatenate([x, x], axis=1)


def sigmoid(x):
    return 1.0 / (1.0 + jnp.exp(-x))


def column(row):
    return jnp.broadcast_to(row, (CHUNK, CHUNK)).T


def fill_masks(seg_ref, mask_ref):
    rows = seg_ref.shape[0]
    seg = seg_ref[...]
    at = lax.broadcasted_iota(jnp.int32, seg.shape, 0)
    for shift in range(1, CONV):
        match = (pltpu.roll(seg, shift, 0) == seg) & (at >= shift)
        mask_ref[shift - 1] = match.astype(F32)


def fill_sums(gamma_ref, sums_ref):
    lane = lax.broadcasted_iota(jnp.int32, (gamma_ref.shape[0], CHUNK), 1)
    for c in range(gamma_ref.shape[1] // CHUNK):
        span = pl.ds(c * CHUNK, CHUNK)
        total = gamma_ref[:, span]
        step = 1
        while step < CHUNK:
            total = total + jnp.where(lane >= step, pltpu.roll(total, step, 1), 0.0)
            step *= 2
        for i in range(gamma_ref.shape[0]):
            sums_ref[i, :, span] = total[i : i + 1]


def wide(mask, columns):
    return mask if columns == CHUNK else twice(mask)


def convolve(x, taps, mask_ref):
    total = x * taps[0:1]
    for shift in range(1, CONV):
        total = total + pltpu.roll(x, shift, 0) * (wide(mask_ref[shift - 1], x.shape[1]) * taps[shift : shift + 1])
    return total


def inverses(systems):
    row = lax.broadcasted_iota(jnp.int32, (CHUNK, CHUNK), 0)
    col = lax.broadcasted_iota(jnp.int32, (CHUNK, CHUNK), 1)
    eye = (row == col).astype(F32)
    near = (row // 2) == (col // 2)
    found = [eye - jnp.where(near, a, 0.0) for a in systems]
    size = 2
    while size < CHUNK:
        part = ((row // (2 * size)) == (col // (2 * size))) & ((row // size) != (col // size))
        packed = [x.astype(BF) for x in found]
        inner = [dot_nn(jnp.where(part, a, 0.0).astype(BF), x).astype(BF) for a, x in zip(systems, packed)]
        found = [x - dot_nn(p, i) for x, p, i in zip(found, packed, inner)]
        size *= 2
    return [x.astype(BF) for x in found]


def chunk_scales(c, h, sums_ref, beta_ref, seg_ref, segrow_ref):
    span = pl.ds(c * CHUNK, CHUNK)
    seg = seg_ref[span, :]
    segrow = segrow_ref[0:1, span]
    sums = sums_ref[h, :, span]
    beta = column(beta_ref[0, :, span])
    down = column(sums)
    row = lax.broadcasted_iota(jnp.int32, (CHUNK, CHUNK), 0)
    col = lax.broadcasted_iota(jnp.int32, (CHUNK, CHUNK), 1)
    same = seg == segrow
    decays = jnp.exp(jnp.where(same & (row >= col), down - sums, -1e30))
    strict = jnp.where(row > col, decays, 0.0)
    ends = jnp.exp(jnp.where(seg == seg[CHUNK - 1 : CHUNK], down[CHUNK - 1 : CHUNK] - down, -1e30))
    if c:
        before = seg_ref[c * CHUNK - 1 : c * CHUNK, :]
        reach = jnp.where(seg == before, jnp.exp(down), 0.0)
    else:
        reach = None
    return beta, decays, strict, ends, reach


def split_head(ref, parts):
    cuts = ((0, DK), (DK, DK), (2 * DK, DV), (2 * DK + DV, DV))[:parts]
    return [ref.at[:, pl.ds(start, size)] for start, size in cuts]


def mix_kernel(
    x_ref, seg_ref, segrow_ref, gamma_ref, beta_ref, tap_ref, gain_ref,
    mixed_ref, out_ref, fresh_ref, inv_ref, state_ref,
    mask_ref, sums_ref,
):
    h = pl.program_id(0)
    q_ref, k_ref, v_ref, gate_ref = split_head(x_ref, 4)
    tapq_ref, tapk_ref, tapv_ref = split_head(tap_ref, 3)

    @pl.when(h == 0)
    def _():
        fill_masks(seg_ref, mask_ref)
        fill_sums(gamma_ref, sums_ref)

    rows = q_ref.shape[0]
    chunks = rows // CHUNK

    def active(ref, tap_ref):
        total = convolve(ref[...].astype(F32), tap_ref[...], mask_ref)
        return total * sigmoid(total)

    q = active(q_ref, tapq_ref).astype(BF)
    kraw = active(k_ref, tapk_ref)
    k = (kraw * lax.rsqrt(jnp.sum(kraw * kraw, axis=-1, keepdims=True) + epsilon)).astype(BF)
    v = active(v_ref, tapv_ref).astype(BF)
    cut = lambda x, c: x[c * CHUNK : (c + 1) * CHUNK]
    scales = [chunk_scales(c, h, sums_ref, beta_ref, seg_ref, segrow_ref) for c in range(chunks)]
    systems = []
    attend = []
    for c in range(chunks):
        beta, decays, strict, ends, reach = scales[c]
        systems.append(beta * strict * dot_nt(cut(k, c), cut(k, c)))
        attend.append((decays * dot_nt(cut(q, c), cut(k, c))).astype(BF))
    found = inverses(systems)
    state = None
    for c in range(chunks):
        beta, decays, strict, ends, reach = scales[c]
        kc, qc, vc = cut(k, c), cut(q, c), cut(v, c).astype(F32)
        inv_ref[0, c] = found[c]
        if c:
            packed = state.astype(BF)
            state_ref[0, c] = packed
            right = twice(beta) * (vc - twice(reach) * dot_nn(kc, packed))
        else:
            state_ref[0, c] = jnp.zeros((DK, DV), BF)
            right = twice(beta) * vc
        fresh = dot_nn(found[c], right.astype(BF)).astype(BF)
        fresh_ref[c * CHUNK : (c + 1) * CHUNK, :] = fresh
        out = dot_nn(attend[c], fresh)
        if c:
            out = out + twice(reach) * dot_nn(qc, packed)
        if c < chunks - 1:
            grown = dot_tn((ends * kc.astype(F32)).astype(BF), fresh)
            state = grown + twice(reach[CHUNK - 1 : CHUNK]) * state if c else grown
        out_ref[c * CHUNK : (c + 1) * CHUNK, :] = out
        unit = out * lax.rsqrt(jnp.mean(out * out, axis=-1, keepdims=True) + out_floor)
        gate = gate_ref[c * CHUNK : (c + 1) * CHUNK, :].astype(F32)
        mixed_ref[c * CHUNK : (c + 1) * CHUNK, :] = (unit * gain_ref[...] * (gate * sigmoid(gate))).astype(BF)


def whole(shape):
    return pl.BlockSpec(shape, lambda h: (0,) * len(shape))


def per_head(rows):
    return pl.BlockSpec((1, 1, rows), lambda h: (h, 0, 0))


def columns(rows, width, at):
    return pl.BlockSpec((rows, width), lambda h: (0, at + h))


HEAD = 2 * DK + 2 * DV
TAPS = 2 * DK + DV


def mixer(projected, at, seg, segrow, gamma, beta, taps, gain):
    rows = projected.shape[0]
    chunks, heads = rows // CHUNK, gamma.shape[0]
    return pl.pallas_call(
        mix_kernel,
        grid=(heads,),
        in_specs=[
            columns(rows, HEAD, at),
            whole((rows, CHUNK)), whole((8, rows)), whole((heads, rows)), per_head(rows),
            columns(CONV, TAPS, at), whole((1, DV)),
        ],
        out_specs=[
            columns(rows, DV, 0), columns(rows, DV, 0), columns(rows, DV, 0),
            pl.BlockSpec((1, chunks, CHUNK, CHUNK), lambda h: (h, 0, 0, 0)),
            pl.BlockSpec((1, chunks, DK, DV), lambda h: (h, 0, 0, 0)),
        ],
        out_shape=[
            jax.ShapeDtypeStruct((rows, heads * DV), BF),
            jax.ShapeDtypeStruct((rows, heads * DV), F32),
            jax.ShapeDtypeStruct((rows, heads * DV), BF),
            jax.ShapeDtypeStruct((heads, chunks, CHUNK, CHUNK), BF),
            jax.ShapeDtypeStruct((heads, chunks, DK, DV), BF),
        ],
        scratch_shapes=[pltpu.VMEM((CONV - 1, rows, CHUNK), F32), pltpu.VMEM((heads, 1, rows), F32)],
        compiler_params=pltpu.CompilerParams(vmem_limit_bytes=32 * 2**20),
        cost_estimate=pl.CostEstimate(flops=heads * int(5e9), bytes_accessed=heads * int(4e6), transcendentals=0),
    )(projected, seg, segrow, gamma, beta[:, None], taps, gain)


def back_kernel(
    x_ref, seg_ref, segrow_ref, gamma_ref, beta_ref, tap_ref, gain_ref,
    out_ref, fresh_ref, inv_ref, state_ref, back_ref, *rest,
):
    dx_ref, dtap_ref, dgain_ref, dgamma_ref, dbeta_ref, mask_ref, sums_ref, lift_ref = rest[-8:]
    h = pl.program_id(0)
    q_ref, k_ref, v_ref, gate_ref = split_head(x_ref, 4)
    tapq_ref, tapk_ref, tapv_ref = split_head(tap_ref, 3)
    dq_ref, dk_ref, dv_ref, dgate_ref = split_head(dx_ref, 4)
    dtapq_ref, dtapk_ref, dtapv_ref = split_head(dtap_ref, 3)

    @pl.when(h == 0)
    def _():
        fill_masks(seg_ref, mask_ref)
        fill_sums(gamma_ref, sums_ref)
        dgain_ref[...] = jnp.zeros_like(dgain_ref)

    rows = q_ref.shape[0]
    chunks = rows // CHUNK

    def active(ref, tap_ref):
        total = convolve(ref[...].astype(F32), tap_ref[...], mask_ref)
        s = sigmoid(total)
        return total * s, s * (1.0 + total * (1.0 - s))

    qf, qslope = active(q_ref, tapq_ref)
    kraw, kslope = active(k_ref, tapk_ref)
    vf, vslope = active(v_ref, tapv_ref)
    kscale = lax.rsqrt(jnp.sum(kraw * kraw, axis=-1, keepdims=True) + epsilon)
    kunit = kraw * kscale
    q, k, v = qf.astype(BF), kunit.astype(BF), vf.astype(BF)
    cut = lambda x, c: x[c * CHUNK : (c + 1) * CHUNK]
    gain = gain_ref[...]
    carried = None
    dqs, dks, dvs = [None] * chunks, [None] * chunks, [None] * chunks
    dgain = jnp.zeros((1, DV), F32)
    for c in reversed(range(chunks)):
        span = pl.ds(c * CHUNK, CHUNK)
        beta, decays, strict, ends, reach = chunk_scales(c, h, sums_ref, beta_ref, seg_ref, segrow_ref)
        kc, qc, vc = cut(k, c), cut(q, c), cut(v, c).astype(F32)
        kcf, qcf = kc.astype(F32), qc.astype(F32)
        out, gate, back = out_ref[span, :], gate_ref[span, :].astype(F32), back_ref[span, :].astype(F32)
        p = lax.rsqrt(jnp.mean(out * out, axis=-1, keepdims=True) + out_floor)
        z = out * p
        s = sigmoid(gate)
        a = back * (gate * s)
        az = a * z
        dgain = dgain + jnp.sum(az, axis=0, keepdims=True)
        dgate_ref[span, :] = (back * (z * gain) * (s * (1.0 + gate * (1.0 - s)))).astype(BF)
        dout = p * (a * gain - z * jnp.mean(az * gain, axis=-1, keepdims=True))
        doutb = dout.astype(BF)
        key_key = dot_nt(kc, kc)
        query_key = dot_nt(qc, kc)
        attend = (decays * query_key).astype(BF)
        fresh = fresh_ref[span, :]
        found = inv_ref[0, c]
        dfresh = dot_tn(attend, doutb)
        if carried is not None:
            carriedb = carried.astype(BF)
            dfresh = dfresh + twice(ends) * dot_nn(kc, carriedb)
        dscore = decays * dot_nt(doutb, fresh)
        dright = dot_tn(found, dfresh.astype(BF))
        drightb = dright.astype(BF)
        dsystem = dot_nt(drightb, fresh)
        dvs[c] = twice(beta) * dright
        m = key_key * (strict * dsystem)
        dkk = (beta * strict) * dsystem
        tally = query_key * dscore - beta * m
        dscoreb = dscore.astype(BF)
        dq = dot_nn(dscoreb, kc)
        dk = dot_tn(dscoreb, qc) - dot_nn((dkk + dkk.T).astype(BF), kc)
        side = tally
        edge = None
        if carried is not None:
            dkf = dot_nt((twice(ends) * fresh.astype(F32)).astype(BF), carriedb)
            dk = dk + dkf
            moved = kcf * dkf
            side = side - moved
            edge = jnp.sum(moved, axis=0, keepdims=True)
        if c:
            state = state_ref[0, c]
            rout = (twice(reach) * dout).astype(BF)
            given = dot_nn(kc, state)
            drest = dright * (vc - twice(reach) * given)
            w = (-twice(beta * reach) * dright).astype(BF)
            dqs1 = dot_nt(rout, state)
            dks1 = dot_nt(w, state)
            dq = dq + dqs1
            dk = dk + dks1
            side = side + qcf * dqs1 + kcf * dks1
            grown = dot_tn(jnp.concatenate([qc, kc], axis=0), jnp.concatenate([rout, w], axis=0))
            if carried is not None:
                last = reach[CHUNK - 1 : CHUNK]
                kept = carried * state.astype(F32)
                edge = edge + last * jnp.sum(kept[:, :CHUNK] + kept[:, CHUNK:], axis=0, keepdims=True)
                carried = twice(last) * carried + grown
            else:
                carried = grown
        else:
            drest = dright * vc
        dqs[c] = dq
        dks[c] = dk
        dbeta = drest[:, :CHUNK] + drest[:, CHUNK:] - m
        dbeta_ref[0, :, span] = jnp.sum(dbeta.T, axis=0, keepdims=True)
        lift = jnp.sum(side.T - tally, axis=0, keepdims=True)
        if edge is not None:
            lane = lax.broadcasted_iota(jnp.int32, (1, CHUNK), 1)
            lift = lift + jnp.where(lane == CHUNK - 1, jnp.sum(edge, axis=1, keepdims=True), 0.0)
        lift_ref[h, :, span] = lift
    dgain_ref[...] += dgain

    def spread(grad, ref, tap_ref, to_ref, dtap_ref):
        x, taps = ref[...].astype(F32), tap_ref[...]
        total = grad * taps[0:1]
        sums = [jnp.sum(grad * x, axis=0, keepdims=True)]
        for shift in range(1, CONV):
            masked = grad * wide(mask_ref[shift - 1], x.shape[1])
            sums.append(jnp.sum(masked * pltpu.roll(x, shift, 0), axis=0, keepdims=True))
            total = total + pltpu.roll(masked, rows - shift, 0) * taps[shift : shift + 1]
        to_ref[...] = total.astype(BF)
        dtap_ref[...] = jnp.concatenate(sums, axis=0)

    spread(jnp.concatenate(dqs, axis=0) * qslope, q_ref, tapq_ref, dq_ref, dtapq_ref)
    dk = jnp.concatenate(dks, axis=0)
    dk = kscale * (dk - kunit * jnp.sum(kunit * dk, axis=-1, keepdims=True))
    spread(dk * kslope, k_ref, tapk_ref, dk_ref, dtapk_ref)
    spread(jnp.concatenate(dvs, axis=0) * vslope, v_ref, tapv_ref, dv_ref, dtapv_ref)

    @pl.when(h == pl.num_programs(0) - 1)
    def _():
        heads = gamma_ref.shape[0]
        lane = lax.broadcasted_iota(jnp.int32, (heads, CHUNK), 1)
        for c in range(chunks):
            span = pl.ds(c * CHUNK, CHUNK)
            total = jnp.concatenate([lift_ref[i, :, span] for i in range(heads)], axis=0)
            step = 1
            while step < CHUNK:
                total = total + jnp.where(lane < CHUNK - step, pltpu.roll(total, CHUNK - step, 1), 0.0)
                step *= 2
            dgamma_ref[:, span] = total


def mixer_back(projected, at, seg, segrow, gamma, beta, taps, gain, out, fresh, inv, state, back, back_at, into):
    rows, width = projected.shape
    chunks, heads = rows // CHUNK, gamma.shape[0]
    given = [] if into is None else [into]
    return pl.pallas_call(
        back_kernel,
        grid=(heads,),
        in_specs=[
            columns(rows, HEAD, at),
            whole((rows, CHUNK)), whole((8, rows)), whole((heads, rows)), per_head(rows),
            columns(CONV, TAPS, at), whole((1, DV)),
            columns(rows, DV, 0), columns(rows, DV, 0),
            pl.BlockSpec((1, chunks, CHUNK, CHUNK), lambda h: (h, 0, 0, 0)),
            pl.BlockSpec((1, chunks, DK, DV), lambda h: (h, 0, 0, 0)),
            columns(rows, DV, back_at),
        ] + [pl.BlockSpec(memory_space=pl.ANY)] * len(given),
        out_specs=[
            columns(rows, HEAD, at), columns(CONV, TAPS, 0),
            whole((1, DV)), whole((heads, rows)), per_head(rows),
        ],
        out_shape=[
            jax.ShapeDtypeStruct((rows, width), BF),
            jax.ShapeDtypeStruct((CONV, heads * TAPS), F32),
            jax.ShapeDtypeStruct((1, DV), F32),
            jax.ShapeDtypeStruct((heads, rows), F32),
            jax.ShapeDtypeStruct((heads, 1, rows), F32),
        ],
        scratch_shapes=[
            pltpu.VMEM((CONV - 1, rows, CHUNK), F32),
            pltpu.VMEM((heads, 1, rows), F32),
            pltpu.VMEM((heads, 1, rows), F32),
        ],
        input_output_aliases={12: 0} if given else {},
        compiler_params=pltpu.CompilerParams(vmem_limit_bytes=32 * 2**20),
        cost_estimate=pl.CostEstimate(flops=heads * int(6e9), bytes_accessed=heads * int(5e6), transcendentals=0),
    )(projected, seg, segrow, gamma, beta[:, None], taps, gain, out, fresh, inv, state, back, *given)


TILE = 256


def ffn_in_kernel(x_ref, gate_w_ref, up_w_ref, gate_ref, up_ref, inner_ref):
    gate, up = dot_nn(x_ref[...], gate_w_ref[...]), dot_nn(x_ref[...], up_w_ref[...])
    gate_ref[...] = gate.astype(BF)
    up_ref[...] = up.astype(BF)
    inner_ref[...] = (gate * sigmoid(gate) * up).astype(BF)


def ffn_in(x, weight):
    rows, depth = x.shape
    width = weight.shape[1] // 2
    tiles = width // TILE
    return pl.pallas_call(
        ffn_in_kernel,
        grid=(tiles,),
        in_specs=[whole((rows, depth)), columns(depth, TILE, 0), columns(depth, TILE, tiles)],
        out_specs=[columns(rows, TILE, 0)] * 3,
        out_shape=[jax.ShapeDtypeStruct((rows, width), BF)] * 3,
        compiler_params=pltpu.CompilerParams(vmem_limit_bytes=32 * 2**20),
        cost_estimate=pl.CostEstimate(flops=4 * rows * depth * width, bytes_accessed=4 * depth * width, transcendentals=0),
    )(x, weight, weight)


def ffn_out_kernel(c_ref, gate_ref, up_ref, inner_ref, down_w_ref, gate_w_ref, up_w_ref, back_ref, down_ref, x_back_ref):
    @pl.when(pl.program_id(0) == 0)
    def _():
        down_ref[...] = jnp.zeros_like(down_ref)
        x_back_ref[...] = jnp.zeros_like(x_back_ref)

    inner_back = dot_nt(c_ref[...], down_w_ref[...])
    gate, up = gate_ref[...].astype(F32), up_ref[...].astype(F32)
    s = sigmoid(gate)
    gate_back = (inner_back * up * (s * (1.0 + gate * (1.0 - s)))).astype(BF)
    up_back = (inner_back * (gate * s)).astype(BF)
    back_ref[0] = gate_back
    back_ref[1] = up_back
    down_ref[...] += dot_nn(inner_ref[...], down_w_ref[...])
    x_back_ref[...] += dot_nt(gate_back, gate_w_ref[...]) + dot_nt(up_back, up_w_ref[...])


def ffn_out(cotangent, gate, up, inner, down_w, gate_up_w):
    rows, width = gate.shape
    depth = cotangent.shape[1]
    tiles = width // TILE
    return pl.pallas_call(
        ffn_out_kernel,
        grid=(tiles,),
        in_specs=[
            whole((rows, depth)),
            columns(rows, TILE, 0), columns(rows, TILE, 0), columns(rows, TILE, 0),
            pl.BlockSpec((TILE, depth), lambda h: (h, 0)),
            columns(depth, TILE, 0), columns(depth, TILE, tiles),
        ],
        out_specs=[pl.BlockSpec((2, rows, TILE), lambda h: (0, 0, h)), whole((rows, depth)), whole((rows, depth))],
        out_shape=[
            jax.ShapeDtypeStruct((2, rows, width), BF),
            jax.ShapeDtypeStruct((rows, depth), F32),
            jax.ShapeDtypeStruct((rows, depth), F32),
        ],
        compiler_params=pltpu.CompilerParams(vmem_limit_bytes=32 * 2**20),
        cost_estimate=pl.CostEstimate(flops=8 * rows * depth * width, bytes_accessed=6 * depth * width, transcendentals=0),
    )(cotangent, gate, up, inner, down_w, gate_up_w, gate_up_w)


SHIFTS = (1, 2, 3)


def place():
    rep = lax.axis_index("rep")
    core, x, y = rep % 2, (rep // 2) % 2, (rep // 4) % 2
    a = jnp.where(core == 0, x, y)
    b = jnp.where(core == 0, y, x)
    return core, a, b


def hop(value, kind):
    count = lax.axis_size("rep")
    if kind == "core":
        pairs = [(i, i ^ 1) for i in range(count)]
    elif kind == "first":
        pairs = [(i, i ^ (4 if i & 1 else 2)) for i in range(count)]
    elif kind == "second":
        pairs = [(i, i ^ (2 if i & 1 else 4)) for i in range(count)]
    else:
        pairs = [(i, i ^ kind) for i in range(count)]
    return lax.ppermute(value, "rep", pairs)


def shift(value, by):
    count = lax.axis_size("shard")
    return lax.ppermute(value, "shard", [(i, (i + by) % count) for i in range(count)])


def after(value, *others):
    if not others:
        return value
    return lax.optimization_barrier((value,) + others)[0]


def assemble_kernel(along, size, rows, cuts, at_ref, own_ref, *refs):
    pieces, whole_ref = refs[:-1], refs[-1]
    to = 0
    for start, width in cuts:
        whole_ref[pl.ds(pl.multiple_of(at_ref[0] * rows, 16), rows), to : to + width] = own_ref[:, start : start + width]
        to += width
    n = 1
    for piece in pieces:
        for slot in range(piece.shape[0]):
            block, part = at_ref[n], at_ref[n + 1]
            n += 2
            if along == 0:
                whole_ref[pl.ds(pl.multiple_of(block * rows + part * size, 16), size), :] = piece[slot]
            else:
                whole_ref[pl.ds(pl.multiple_of(block * rows, 16), rows), pl.ds(pl.multiple_of(part * size, 128), size)] = piece[slot]


class Gather:
    def __init__(self, weight, along, cuts=None, blocks=None):
        self.weight, self.along, self.blocks = weight, along, blocks
        self.cuts = cuts or [(0, weight.shape[1])]
        self.width = sum(width for _, width in self.cuts)
        self.size = (weight.shape[0], self.width)[along] // 8

    def deep(self, *tokens):
        core, a, b = place()
        part = core * 4 + a * 2 + b
        if self.blocks is None:
            mine = lax.dynamic_slice_in_dim(self.weight, part * self.size, self.size, self.along)
        else:
            mine = jnp.concatenate([pick(self.weight, n, 128, 1) for n in self.blocks(part)], axis=1)
        mine = after(mine, *tokens)
        self.raw = [shift(mine, by) for by in range(1, lax.axis_size("shard"))]

    def first(self, *tokens):
        count = len(self.raw)
        raw = lax.optimization_barrier(tuple(self.raw) + tokens)[:count]
        self.here = jnp.stack(raw)
        self.come = hop(self.here, "first")

    def second(self, *tokens):
        self.pair = jnp.concatenate([self.here, after(self.come, *tokens)])
        self.others = hop(self.pair, "second")
        self.pair_core = hop(self.pair, "core")

    def core(self, *tokens):
        self.others_in = after(self.others, *tokens)
        self.others_core = hop(self.others_in, "core")

    def full(self, *tokens):
        core, a, b = place()
        z, count = lax.axis_index("shard"), lax.axis_size("shard")
        part, other = core * 4 + a * 2 + b, (1 - core) * 4 + b * 2 + a
        blocks = [(z - by) % count for by in range(1, count)]
        at = [z]
        for home, flips in ((part, (0, 2)), (part, (1, 3)), (other, (0, 2)), (other, (1, 3))):
            for flip in flips:
                for block in blocks:
                    at += [block, home ^ flip]
        rows, width = self.weight.shape[0], self.width
        pieces = [self.pair, self.others_in, self.pair_core, after(self.others_core, *tokens)]
        return pl.pallas_call(
            functools.partial(assemble_kernel, self.along, self.size, rows, self.cuts),
            in_specs=[pl.BlockSpec(memory_space=pltpu.SMEM)] + [pl.BlockSpec(memory_space=pltpu.VMEM)] * 5,
            out_specs=pl.BlockSpec(memory_space=pltpu.VMEM),
            compiler_params=pltpu.CompilerParams(vmem_limit_bytes=48 * 2**20),
            out_shape=jax.ShapeDtypeStruct((rows * count, width), BF),
        )(jnp.stack(at).astype(jnp.int32), self.weight, *pieces)


def pick(value, at, size, axis):
    return lax.dynamic_slice_in_dim(value, at * size, size, axis)


def join(bit, mine, theirs, axis):
    return jnp.where(bit == 0, jnp.concatenate([mine, theirs], axis), jnp.concatenate([theirs, mine], axis))


class Total:
    def __init__(self, left, right):
        self.left, self.right = left, right
        self.count = lax.axis_size("shard")
        self.rows = left.shape[1] // self.count
        self.quarter = right.size // right.shape[-2] // 4

    def core(self, *tokens):
        core, a, b = place()
        half = 2 * self.quarter
        right = after(self.right, *tokens) if tokens else self.right
        if right.ndim == 3:
            self.own, other = (pick(right, n, 1, 0)[0] for n in (core, 1 - core))
        else:
            self.own, other = (pick(right, n, half, 1) for n in (core, 1 - core))
        self.given = dot_tn(self.left, other).astype(BF)
        self.got = hop(self.given, "core")
        return self.got

    def first(self, *tokens):
        core, a, b = place()
        self.got = after(self.got, *tokens)
        sent = dot_tn(self.left, pick(self.own, 1 - a, self.quarter, 1)) + pick(self.got, 1 - a, self.quarter, 1).astype(F32)
        self.sent = sent.astype(BF)
        self.got_first = hop(self.sent, "first")

    def second(self, *tokens):
        core, a, b = place()
        got_first = after(self.got_first, *tokens)
        kept = dot_tn(self.left, pick(self.own, a, self.quarter, 1)) + pick(self.got, a, self.quarter, 1).astype(F32)
        kept = (kept + got_first.astype(F32)).astype(BF).reshape(self.count, self.rows, self.quarter)
        self.axis = 2 if self.quarter % 256 == 0 else 1
        size = kept.shape[self.axis] // 2
        self.passed = pick(kept, 1 - b, size, self.axis)
        self.mine = pick(kept, b, size, self.axis)
        self.got_second = hop(self.passed, "second")

    def deep(self, *tokens):
        z = lax.axis_index("shard")
        kept = (self.mine.astype(F32) + after(self.got_second, *tokens).astype(F32)).astype(BF)
        extra = 8
        while extra < lax.axis_size("rep"):
            kept = (kept.astype(F32) + hop(kept, extra).astype(F32)).astype(BF)
            extra *= 2
        self.kept = kept
        self.raw = [shift(pick(kept, (z + by) % self.count, 1, 0)[0], by) for by in range(1, self.count)]

    def finish(self, *tokens):
        total = pick(self.kept, lax.axis_index("shard"), 1, 0)[0].astype(F32)
        for piece in lax.optimization_barrier(tuple(self.raw) + tokens)[: len(self.raw)]:
            total = total + piece.astype(F32)
        self.done = total.astype(BF)


def final_kernel(copies, at_ref, *refs):
    pieces, outs = refs[:8], refs[8:]
    n = 0
    for piece in pieces:
        for start, size, width, out, moving, fixed in copies:
            block = piece[start : start + size, :width].astype(F32)
            if moving == "both":
                rows = pl.ds(pl.multiple_of(at_ref[n] * size, 8), size)
                outs[out][rows, pl.ds(pl.multiple_of(at_ref[n + 1] * 128, 128), width)] = block
                n += 2
            else:
                outs[out][:, pl.ds(pl.multiple_of(at_ref[n] * 128, 128), width)] = block
                n += 1


class Spread:
    def __init__(self, done):
        self.done = done
        self.theirs = hop(done, "second")

    def first(self, *tokens):
        self.pair = jnp.stack([self.done, after(self.theirs, *tokens)])
        self.others = hop(self.pair, "first")

    def core(self, *tokens):
        self.four = jnp.concatenate([self.pair, after(self.others, *tokens)])
        self.over = hop(self.four, "core")

    def parts(self, *tokens):
        over = after(self.over, *tokens)
        return [self.four[n] for n in range(4)] + [over[n] for n in range(4)]


def part_numbers():
    core, a, b = place()
    home, away = core * 4 + a * 2 + b, (1 - core) * 4 + b * 2 + a
    return [home ^ n for n in range(4)] + [away ^ n for n in range(4)]


def finish_totals(pieces, copies, at, shapes):
    return pl.pallas_call(
        functools.partial(final_kernel, copies),
        in_specs=[pl.BlockSpec(memory_space=pltpu.SMEM)] + [pl.BlockSpec(memory_space=pltpu.VMEM)] * 8,
        out_specs=[pl.BlockSpec(memory_space=pltpu.VMEM)] * len(shapes),
        compiler_params=pltpu.CompilerParams(vmem_limit_bytes=48 * 2**20),
        out_shape=[jax.ShapeDtypeStruct(s, F32) for s in shapes],
    )(jnp.stack(at).astype(jnp.int32), *pieces)


def rms_scale(values, gain):
    return values * lax.rsqrt(jnp.mean(values * values, axis=-1, keepdims=True) + epsilon) * gain


def as_rows(x, count):
    flat = x.astype(F32).reshape(count, -1)
    return jnp.pad(flat, ((0, 0), (0, -flat.shape[1] % 1024))).reshape(count, -1, 128)


def from_rows(rows, shapes):
    found, start = [], 0
    for shape in shapes:
        size = math.prod(shape)
        deep = -(-size // 1024) * 8
        piece = rows[:, start : start + deep].reshape(rows.shape[0], -1)[:, :size]
        found.append(piece.reshape((rows.shape[0],) + shape))
        start += deep
    return found


def share_small(arrays, *tokens):
    count = lax.axis_size("shard")
    z = lax.axis_index("shard")
    flat = after(jnp.concatenate([as_rows(x, 1) for x in arrays], axis=1), *tokens)
    every = jnp.zeros((count,) + flat.shape[1:], F32)
    every = lax.dynamic_update_slice_in_dim(every, flat, z, 0)
    for by in range(1, count):
        every = lax.dynamic_update_slice_in_dim(every, shift(flat, by), (z - by) % count, 0)
    return from_rows(every, [x.shape for x in arrays])


class Small:
    def __init__(self, arrays):
        self.shapes = [x.shape[1:] for x in arrays]
        count, z = lax.axis_size("shard"), lax.axis_index("shard")
        flat = jnp.concatenate([as_rows(x, count) for x in arrays], axis=1)
        self.total = pick(flat, z, 1, 0)
        self.raw = [shift(pick(flat, (z + by) % count, 1, 0), by) for by in range(1, count)]
        self.step = 1

    def add(self, *tokens):
        for piece in lax.optimization_barrier(tuple(self.raw) + tokens)[: len(self.raw)]:
            self.total = self.total + piece
        if self.step < lax.axis_size("rep"):
            self.raw = [hop(self.total, self.step)]
            self.step *= 2
        else:
            self.raw = []

    def finish(self):
        while self.raw:
            self.add()
        return [x[0] for x in from_rows(self.total, self.shapes)]


def beside(blocks):
    return jnp.concatenate(list(blocks), axis=-1)


def parted(x):
    count = lax.axis_size("shard")
    return jnp.moveaxis(x.reshape(x.shape[:-1] + (count, -1)), -2, 0)


GROUPS = 2
STEPS = 4


def group_cuts(g):
    cuts = []
    for h in range(g * HEADS // GROUPS, (g + 1) * HEADS // GROUPS):
        cuts += [(h * DK, DK), (KEYS + h * DK, DK), (2 * KEYS + h * DV, DV), (2 * KEYS + VALS + h * DV, DV)]
    return cuts


def group_blocks(g, part):
    each, found = HEAD * HEADS // GROUPS // 8 // 128, []
    for n in range(each):
        block = (part + 8 * g) * each + n
        head, slot = block // (HEAD // 128), block % (HEAD // 128)
        to = jnp.where(slot < 2, slot * HEADS + head, 2 * HEADS + 2 * head + slot - 2)
        found.append(jnp.where(slot < 4, to, 4 * HEADS + 2 * head + slot - 4))
    return found


def mix_final_kernel(blocks, at_ref, *refs):
    for n, piece in enumerate(refs[:-1]):
        for m in range(blocks):
            to = pl.ds(pl.multiple_of(at_ref[n * blocks + m] * 128, 128), 128)
            refs[-1][:, to] = piece[:, m * 128 : (m + 1) * 128].astype(F32)


def finish_mix(pieces, blocks, at, shape):
    return pl.pallas_call(
        functools.partial(mix_final_kernel, blocks),
        in_specs=[pl.BlockSpec(memory_space=pltpu.SMEM)] + [pl.BlockSpec(memory_space=pltpu.VMEM)] * len(pieces),
        out_specs=pl.BlockSpec(memory_space=pltpu.VMEM),
        compiler_params=pltpu.CompilerParams(vmem_limit_bytes=48 * 2**20),
        out_shape=jax.ShapeDtypeStruct(shape, F32),
    )(jnp.stack(at).astype(jnp.int32), *pieces)


def body(
    hidden_in,
    segment_ids,
    norm_gains,
    w_mix_in,
    w_decay,
    decay_params,
    conv_weight,
    out_gain,
    w_mix_out,
    w_gate_up,
    w_down,
    cotangent,
):
    rows = hidden_in.shape[0]
    ga, gb = (
        Gather(w_mix_in, 1, group_cuts(g), functools.partial(group_blocks, g)) for g in range(GROUPS)
    )
    go, gu, gd = Gather(w_mix_out, 1), Gather(w_gate_up, 0), Gather(w_down, 1)
    ga.deep()
    ga.first()
    gb.deep(*ga.raw)
    ga.second(*gb.raw)
    go.deep(*gb.raw)
    ga.core(*go.raw)

    small = share_small([norm_gains, decay_params, conv_weight, out_gain[None], w_decay], ga.raw[0])
    gains, rates, taps, gain_row = (beside(x) for x in small[:4])
    decay_full = small[4].reshape(-1, 2 * HEADS).astype(BF)

    hidden = hidden_in.astype(F32)
    normed_one_f, norm_one_pull = jax.vjp(rms_scale, hidden, gains[0])
    normed_one = normed_one_f.astype(BF)
    logits = dot_nt(decay_full.T, normed_one)
    rate, bias = jnp.exp(rates[0])[:, None], rates[1][:, None]
    gamma = -rate * jax.nn.softplus(logits[:HEADS] + bias)
    beta = jax.nn.sigmoid(logits[HEADS:])
    seg = jnp.broadcast_to(segment_ids[:, None], (rows, CHUNK))
    segrow = jnp.broadcast_to(segment_ids[None], (8, rows))
    cuts = (taps[:, :KEYS], taps[:, KEYS : 2 * KEYS], taps[:, 2 * KEYS :])
    by_head = jnp.concatenate([x.reshape(CONV, HEADS, -1) for x in cuts], axis=2).reshape(CONV, -1)
    tap_groups = jnp.split(by_head, GROUPS, axis=1)
    heads = HEADS // STEPS

    mix_in = [ga.full(), None]
    gb.first(mix_in[0])
    projected = [dot_nn(normed_one, mix_in[0]), None]
    gb.second(projected[0])
    gu.deep(mix_in[0])
    kept = []

    def mix(n, *tokens):
        g, at = n * GROUPS // STEPS, n % (STEPS // GROUPS) * heads
        span = slice(n * heads, (n + 1) * heads)
        gate = after(gamma[span], *tokens) if tokens else gamma[span]
        kept.append(mixer(projected[g], at, seg, segrow, gate, beta[span], tap_groups[g], gain_row))
        return kept[-1][0]

    done = mix(0)
    gb.core(done)
    done = mix(1, gu.raw[0])
    mix_in[1] = gb.full(done)
    go.first(done)
    projected[1] = dot_nn(after(normed_one, done, gu.raw[1]), mix_in[1])
    go.second(projected[1])
    gu.first(projected[1])
    gd.deep(projected[1], *gu.raw)
    done = mix(2, gu.here, go.pair)
    gu.second(done)
    go.core(done)
    done = mix(3, gu.pair, gd.raw[0])
    gd.first(done)
    mix_out = go.full()
    mixed_out = jnp.concatenate([x[0] for x in kept], axis=1)
    residual = hidden + dot_nn(mixed_out, mix_out)
    normed_two_f, norm_two_pull = jax.vjp(rms_scale, residual, gains[1])
    normed_two = normed_two_f.astype(BF)
    gu.core(normed_two)
    gate_up_full = gu.full()
    gd.second(gate_up_full)
    gate, up, inner = ffn_in(after(normed_two, gd.pair), gate_up_full)
    gd.core(inner)
    down_full = gd.full()
    t_down = Total(inner, cotangent)
    t_down.core()
    gate_up_back, down, normed_two_back = ffn_out(
        after(cotangent, t_down.given), gate, up, inner, down_full, gate_up_full
    )
    t_gu = Total(normed_two, gate_up_back)
    t_gu.core()
    t_down.first(t_gu.given)
    result = (residual + down).astype(BF)
    residual_part, gain_two = norm_two_pull(after(normed_two_back, t_down.sent))
    t_gu.first(gain_two)
    residual_back = cotangent.astype(F32) + residual_part
    branch_back = after(residual_back.astype(BF), t_gu.sent)
    t_out = Total(mixed_out, branch_back)
    t_out.core()
    mixed_back = dot_nt(branch_back, mix_out)

    backs = []

    def mix_back(n, *tokens):
        g, at = n * GROUPS // STEPS, n % (STEPS // GROUPS) * heads
        span = slice(n * heads, (n + 1) * heads)
        gate = after(gamma[span], *tokens)
        into = backs[-1][0] if at else None
        backs.append(
            mixer_back(
                projected[g], at, seg, segrow, gate, beta[span], tap_groups[g], gain_row, *kept[n][1:], mixed_back, n * heads, into
            )
        )
        return backs[-1][0]

    done = mix_back(0, t_gu.sent, t_out.given)
    t_out.first(done)
    t_down.second(done)
    done = mix_back(1, t_out.sent, t_down.passed)
    back_a = done
    t_a = Total(normed_one, back_a)
    t_a.core(done)
    t_down.deep(done)
    done = mix_back(2, t_a.given, t_down.kept)
    t_gu.second(done)
    t_a.first(t_gu.passed)
    t_out.second(t_a.sent)
    done = mix_back(3, t_a.sent, t_out.passed)
    t_down.finish(done)
    back_b = done
    t_b = Total(normed_one, back_b)
    t_b.core(done)
    t_gu.deep(t_b.given)
    t_out.deep(t_gu.kept)
    dgain = sum(x[2] for x in backs)
    dgamma = jnp.concatenate([x[3] for x in backs], axis=0)
    dbeta = jnp.concatenate([x[4][:, 0] for x in backs], axis=0)
    slope = -dgamma * rate * jax.nn.sigmoid(logits[:HEADS] + bias)
    logits_back = jnp.concatenate([slope, dbeta * beta * (1.0 - beta)], axis=0).astype(BF)
    grad_rates = jnp.stack([jnp.sum(dgamma * gamma, axis=1), jnp.sum(slope, axis=1)])
    by_head = jnp.concatenate([x[1] for x in backs], axis=1).reshape(CONV, HEADS, TAPS)
    cuts = (by_head[:, :, :DK], by_head[:, :, DK : 2 * DK], by_head[:, :, 2 * DK :])
    grad_taps = jnp.concatenate([x.reshape(CONV, -1) for x in cuts], axis=1)
    grad_decay = lax.dot_general(normed_one, logits_back, (((0,), (1,)), ((), ())), preferred_element_type=F32)
    t_b.first()
    near = lax.dot_general(logits_back, decay_full, (((0,), (1,)), ((), ())), preferred_element_type=F32)
    near = near + dot_nt(after(back_a, t_b.sent), mix_in[0]) + dot_nt(back_b, mix_in[1])
    t_a.second(near)
    hidden_part, gain_one = norm_one_pull(after(near, t_a.passed))
    grad_in = residual_back + hidden_part
    t_b.second(gain_one)
    t_a.deep(t_b.passed)
    t_gu.finish(t_b.passed)
    t_out.finish(t_b.passed)
    count = lax.axis_size("shard")
    small_total = Small([
        parted(jnp.stack([gain_one, gain_two])),
        grad_decay.reshape(count, -1, 2 * HEADS),
        parted(grad_rates),
        parted(grad_taps),
        parted(dgain[0]),
    ])
    numbers = part_numbers()
    wide = t_gu.done.shape[1] // 128
    merged = jnp.concatenate(
        [t_down.done, t_out.done] + [t_gu.done[:, n * 128 : (n + 1) * 128] for n in range(wide)]
    )
    s_rest = Spread(merged)
    t_b.deep(s_rest.done)
    small_total.add(t_b.kept)
    s_rest.first(t_b.raw[0])
    t_a.finish(s_rest.pair)
    t_b.finish(s_rest.pair)
    s_mix = Spread(jnp.concatenate([t_a.done, t_b.done], axis=1))
    small_total.add(s_mix.done)
    s_rest.core(s_mix.done)
    s_mix.first(s_rest.four)
    small_total.add(s_mix.pair)
    copies, at, start = [], [], 0
    for out, deep in enumerate((t_down.rows, t_out.rows)):
        copies.append((start, deep, 128, out, "columns", 0))
        start += deep
    for n in range(wide):
        copies.append((start, t_gu.rows // 2, 128, 2, "both", n))
        start += t_gu.rows // 2
    for part in numbers:
        at += [part, part]
        for n in range(wide):
            at += [part % 2, part // 2 * wide + n]
    grad_down, grad_mix_out, grad_gate_up = finish_totals(
        s_rest.parts(s_mix.pair), copies, at, [w_down.shape, w_mix_out.shape, w_gate_up.shape]
    )
    s_mix.core(grad_down)
    small_total.add(s_mix.four)
    parts = small_total.finish()
    each = t_a.done.shape[1] // 128
    copies, at = [], []
    for part in numbers:
        for g in range(GROUPS):
            at += group_blocks(g, part)
    pieces = s_mix.parts()
    grad_mix_in = finish_mix(pieces, GROUPS * each, at, w_mix_in.shape)
    return (
        result,
        grad_in,
        parts[0],
        grad_mix_in,
        parts[1],
        parts[2],
        parts[3],
        parts[4],
        grad_mix_out,
        grad_gate_up,
        grad_down,
    )


def solution(mesh):
    rows, columns_, both = P("shard", None), P(None, "shard"), P(("rep", "shard"), None)
    return jax.shard_map(
        body,
        mesh=mesh,
        in_specs=(both, P(("rep", "shard")), columns_, rows, rows, columns_, columns_, P("shard"), rows, rows, rows, both),
        out_specs=(both, both, columns_, rows, rows, columns_, columns_, P("shard"), rows, rows, rows),
        check_vma=False,
    )
```

```python
import functools
import math

import jax
import jax.numpy as jnp
from jax import lax
from jax.experimental import pallas as pl
from jax.experimental.pallas import tpu as pltpu
from jax.sharding import PartitionSpec as P

HEADS = 8
DK = 128
DV = 256
FF = 2816
CONV = 4
KEYS = 1024
VALS = 2048
CHUNK = 128
epsilon = 1e-06
out_floor = 0.01
BF = jnp.bfloat16
F32 = jnp.float32


def dot_nn(a, b):
    return jnp.dot(a, b, preferred_element_type=F32)


def dot_nt(a, b):
    return lax.dot_general(a, b, (((1,), (1,)), ((), ())), preferred_element_type=F32)


def dot_tn(a, b):
    return lax.dot_general(a, b, (((0,), (0,)), ((), ())), preferred_element_type=F32)


def twice(x):
    return jnp.concatenate([x, x], axis=1)


def sigmoid(x):
    return 1.0 / (1.0 + jnp.exp(-x))


def column(row):
    return jnp.broadcast_to(row, (CHUNK, CHUNK)).T


def fill_masks(seg_ref, mask_ref):
    rows = seg_ref.shape[0]
    seg = seg_ref[...]
    at = lax.broadcasted_iota(jnp.int32, seg.shape, 0)
    for shift in range(1, CONV):
        match = (pltpu.roll(seg, shift, 0) == seg) & (at >= shift)
        mask_ref[shift - 1] = match.astype(F32)


def fill_sums(gamma_ref, sums_ref):
    lane = lax.broadcasted_iota(jnp.int32, (gamma_ref.shape[0], CHUNK), 1)
    for c in range(gamma_ref.shape[1] // CHUNK):
        span = pl.ds(c * CHUNK, CHUNK)
        total = gamma_ref[:, span]
        step = 1
        while step < CHUNK:
            total = total + jnp.where(lane >= step, pltpu.roll(total, step, 1), 0.0)
            step *= 2
        for i in range(gamma_ref.shape[0]):
            sums_ref[i, :, span] = total[i : i + 1]


def wide(mask, columns):
    return mask if columns == CHUNK else twice(mask)


def convolve(x, taps, mask_ref):
    total = x * taps[0:1]
    for shift in range(1, CONV):
        total = total + pltpu.roll(x, shift, 0) * (wide(mask_ref[shift - 1], x.shape[1]) * taps[shift : shift + 1])
    return total


def inverses(systems):
    row = lax.broadcasted_iota(jnp.int32, (CHUNK, CHUNK), 0)
    col = lax.broadcasted_iota(jnp.int32, (CHUNK, CHUNK), 1)
    eye = (row == col).astype(F32)
    near = (row // 2) == (col // 2)
    found = [eye - jnp.where(near, a, 0.0) for a in systems]
    size = 2
    while size < CHUNK:
        part = ((row // (2 * size)) == (col // (2 * size))) & ((row // size) != (col // size))
        packed = [x.astype(BF) for x in found]
        inner = [dot_nn(jnp.where(part, a, 0.0).astype(BF), x).astype(BF) for a, x in zip(systems, packed)]
        found = [x - dot_nn(p, i) for x, p, i in zip(found, packed, inner)]
        size *= 2
    return [x.astype(BF) for x in found]


def chunk_scales(c, h, sums_ref, beta_ref, seg_ref, segrow_ref):
    span = pl.ds(c * CHUNK, CHUNK)
    seg = seg_ref[span, :]
    segrow = segrow_ref[0:1, span]
    sums = sums_ref[h, :, span]
    beta = column(beta_ref[0, :, span])
    down = column(sums)
    row = lax.broadcasted_iota(jnp.int32, (CHUNK, CHUNK), 0)
    col = lax.broadcasted_iota(jnp.int32, (CHUNK, CHUNK), 1)
    same = seg == segrow
    decays = jnp.exp(jnp.where(same & (row >= col), down - sums, -1e30))
    strict = jnp.where(row > col, decays, 0.0)
    ends = jnp.exp(jnp.where(seg == seg[CHUNK - 1 : CHUNK], down[CHUNK - 1 : CHUNK] - down, -1e30))
    if c:
        before = seg_ref[c * CHUNK - 1 : c * CHUNK, :]
        reach = jnp.where(seg == before, jnp.exp(down), 0.0)
    else:
        reach = None
    return beta, decays, strict, ends, reach


def split_head(ref, parts):
    cuts = ((0, DK), (DK, DK), (2 * DK, DV), (2 * DK + DV, DV))[:parts]
    return [ref.at[:, pl.ds(start, size)] for start, size in cuts]


def mix_kernel(
    x_ref, seg_ref, segrow_ref, gamma_ref, beta_ref, tap_ref, gain_ref,
    mixed_ref, out_ref, fresh_ref, inv_ref, state_ref,
    mask_ref, sums_ref,
):
    h = pl.program_id(0)
    q_ref, k_ref, v_ref, gate_ref = split_head(x_ref, 4)
    tapq_ref, tapk_ref, tapv_ref = split_head(tap_ref, 3)

    @pl.when(h == 0)
    def _():
        fill_masks(seg_ref, mask_ref)
        fill_sums(gamma_ref, sums_ref)

    rows = q_ref.shape[0]
    chunks = rows // CHUNK

    def active(ref, tap_ref):
        total = convolve(ref[...].astype(F32), tap_ref[...], mask_ref)
        return total * sigmoid(total)

    q = active(q_ref, tapq_ref).astype(BF)
    kraw = active(k_ref, tapk_ref)
    k = (kraw * lax.rsqrt(jnp.sum(kraw * kraw, axis=-1, keepdims=True) + epsilon)).astype(BF)
    v = active(v_ref, tapv_ref).astype(BF)
    cut = lambda x, c: x[c * CHUNK : (c + 1) * CHUNK]
    scales = [chunk_scales(c, h, sums_ref, beta_ref, seg_ref, segrow_ref) for c in range(chunks)]
    systems = []
    attend = []
    for c in range(chunks):
        beta, decays, strict, ends, reach = scales[c]
        systems.append(beta * strict * dot_nt(cut(k, c), cut(k, c)))
        attend.append((decays * dot_nt(cut(q, c), cut(k, c))).astype(BF))
    found = inverses(systems)
    state = None
    for c in range(chunks):
        beta, decays, strict, ends, reach = scales[c]
        kc, qc, vc = cut(k, c), cut(q, c), cut(v, c).astype(F32)
        inv_ref[0, c] = found[c]
        if c:
            packed = state.astype(BF)
            state_ref[0, c] = packed
            right = twice(beta) * (vc - twice(reach) * dot_nn(kc, packed))
        else:
            state_ref[0, c] = jnp.zeros((DK, DV), BF)
            right = twice(beta) * vc
        fresh = dot_nn(found[c], right.astype(BF)).astype(BF)
        fresh_ref[c * CHUNK : (c + 1) * CHUNK, :] = fresh
        out = dot_nn(attend[c], fresh)
        if c:
            out = out + twice(reach) * dot_nn(qc, packed)
        if c < chunks - 1:
            grown = dot_tn((ends * kc.astype(F32)).astype(BF), fresh)
            state = grown + twice(reach[CHUNK - 1 : CHUNK]) * state if c else grown
        out_ref[c * CHUNK : (c + 1) * CHUNK, :] = out
        unit = out * lax.rsqrt(jnp.mean(out * out, axis=-1, keepdims=True) + out_floor)
        gate = gate_ref[c * CHUNK : (c + 1) * CHUNK, :].astype(F32)
        mixed_ref[c * CHUNK : (c + 1) * CHUNK, :] = (unit * gain_ref[...] * (gate * sigmoid(gate))).astype(BF)


def whole(shape):
    return pl.BlockSpec(shape, lambda h: (0,) * len(shape))


def per_head(rows):
    return pl.BlockSpec((1, 1, rows), lambda h: (h, 0, 0))


def columns(rows, width, at):
    return pl.BlockSpec((rows, width), lambda h: (0, at + h))


HEAD = 2 * DK + 2 * DV
TAPS = 2 * DK + DV


def mixer(projected, at, seg, segrow, gamma, beta, taps, gain):
    rows = projected.shape[0]
    chunks, heads = rows // CHUNK, gamma.shape[0]
    return pl.pallas_call(
        mix_kernel,
        grid=(heads,),
        in_specs=[
            columns(rows, HEAD, at),
            whole((rows, CHUNK)), whole((8, rows)), whole((heads, rows)), per_head(rows),
            columns(CONV, TAPS, at), whole((1, DV)),
        ],
        out_specs=[
            columns(rows, DV, 0), columns(rows, DV, 0), columns(rows, DV, 0),
            pl.BlockSpec((1, chunks, CHUNK, CHUNK), lambda h: (h, 0, 0, 0)),
            pl.BlockSpec((1, chunks, DK, DV), lambda h: (h, 0, 0, 0)),
        ],
        out_shape=[
            jax.ShapeDtypeStruct((rows, heads * DV), BF),
            jax.ShapeDtypeStruct((rows, heads * DV), F32),
            jax.ShapeDtypeStruct((rows, heads * DV), BF),
            jax.ShapeDtypeStruct((heads, chunks, CHUNK, CHUNK), BF),
            jax.ShapeDtypeStruct((heads, chunks, DK, DV), BF),
        ],
        scratch_shapes=[pltpu.VMEM((CONV - 1, rows, CHUNK), F32), pltpu.VMEM((heads, 1, rows), F32)],
        compiler_params=pltpu.CompilerParams(vmem_limit_bytes=32 * 2**20),
        cost_estimate=pl.CostEstimate(flops=heads * int(5e9), bytes_accessed=heads * int(4e6), transcendentals=0),
    )(projected, seg, segrow, gamma, beta[:, None], taps, gain)


def back_kernel(
    x_ref, seg_ref, segrow_ref, gamma_ref, beta_ref, tap_ref, gain_ref,
    out_ref, fresh_ref, inv_ref, state_ref, back_ref, *rest,
):
    dx_ref, dtap_ref, dgain_ref, dgamma_ref, dbeta_ref, mask_ref, sums_ref, lift_ref = rest[-8:]
    h = pl.program_id(0)
    q_ref, k_ref, v_ref, gate_ref = split_head(x_ref, 4)
    tapq_ref, tapk_ref, tapv_ref = split_head(tap_ref, 3)
    dq_ref, dk_ref, dv_ref, dgate_ref = split_head(dx_ref, 4)
    dtapq_ref, dtapk_ref, dtapv_ref = split_head(dtap_ref, 3)

    @pl.when(h == 0)
    def _():
        fill_masks(seg_ref, mask_ref)
        fill_sums(gamma_ref, sums_ref)
        dgain_ref[...] = jnp.zeros_like(dgain_ref)

    rows = q_ref.shape[0]
    chunks = rows // CHUNK

    def active(ref, tap_ref):
        total = convolve(ref[...].astype(F32), tap_ref[...], mask_ref)
        s = sigmoid(total)
        return total * s, s * (1.0 + total * (1.0 - s))

    qf, qslope = active(q_ref, tapq_ref)
    kraw, kslope = active(k_ref, tapk_ref)
    vf, vslope = active(v_ref, tapv_ref)
    kscale = lax.rsqrt(jnp.sum(kraw * kraw, axis=-1, keepdims=True) + epsilon)
    kunit = kraw * kscale
    q, k, v = qf.astype(BF), kunit.astype(BF), vf.astype(BF)
    cut = lambda x, c: x[c * CHUNK : (c + 1) * CHUNK]
    gain = gain_ref[...]
    carried = None
    dqs, dks, dvs = [None] * chunks, [None] * chunks, [None] * chunks
    dgain = jnp.zeros((1, DV), F32)
    for c in reversed(range(chunks)):
        span = pl.ds(c * CHUNK, CHUNK)
        beta, decays, strict, ends, reach = chunk_scales(c, h, sums_ref, beta_ref, seg_ref, segrow_ref)
        kc, qc, vc = cut(k, c), cut(q, c), cut(v, c).astype(F32)
        kcf, qcf = kc.astype(F32), qc.astype(F32)
        out, gate, back = out_ref[span, :], gate_ref[span, :].astype(F32), back_ref[span, :].astype(F32)
        p = lax.rsqrt(jnp.mean(out * out, axis=-1, keepdims=True) + out_floor)
        z = out * p
        s = sigmoid(gate)
        a = back * (gate * s)
        az = a * z
        dgain = dgain + jnp.sum(az, axis=0, keepdims=True)
        dgate_ref[span, :] = (back * (z * gain) * (s * (1.0 + gate * (1.0 - s)))).astype(BF)
        dout = p * (a * gain - z * jnp.mean(az * gain, axis=-1, keepdims=True))
        doutb = dout.astype(BF)
        key_key = dot_nt(kc, kc)
        query_key = dot_nt(qc, kc)
        attend = (decays * query_key).astype(BF)
        fresh = fresh_ref[span, :]
        found = inv_ref[0, c]
        dfresh = dot_tn(attend, doutb)
        if carried is not None:
            carriedb = carried.astype(BF)
            dfresh = dfresh + twice(ends) * dot_nn(kc, carriedb)
        dscore = decays * dot_nt(doutb, fresh)
        dright = dot_tn(found, dfresh.astype(BF))
        drightb = dright.astype(BF)
        dsystem = dot_nt(drightb, fresh)
        dvs[c] = twice(beta) * dright
        m = key_key * (strict * dsystem)
        dkk = (beta * strict) * dsystem
        tally = query_key * dscore - beta * m
        dscoreb = dscore.astype(BF)
        dq = dot_nn(dscoreb, kc)
        dk = dot_tn(dscoreb, qc) - dot_nn((dkk + dkk.T).astype(BF), kc)
        side = tally
        edge = None
        if carried is not None:
            dkf = dot_nt((twice(ends) * fresh.astype(F32)).astype(BF), carriedb)
            dk = dk + dkf
            moved = kcf * dkf
            side = side - moved
            edge = jnp.sum(moved, axis=0, keepdims=True)
        if c:
            state = state_ref[0, c]
            rout = (twice(reach) * dout).astype(BF)
            given = dot_nn(kc, state)
            drest = dright * (vc - twice(reach) * given)
            w = (-twice(beta * reach) * dright).astype(BF)
            dqs1 = dot_nt(rout, state)
            dks1 = dot_nt(w, state)
            dq = dq + dqs1
            dk = dk + dks1
            side = side + qcf * dqs1 + kcf * dks1
            grown = dot_tn(jnp.concatenate([qc, kc], axis=0), jnp.concatenate([rout, w], axis=0))
            if carried is not None:
                last = reach[CHUNK - 1 : CHUNK]
                kept = carried * state.astype(F32)
                edge = edge + last * jnp.sum(kept[:, :CHUNK] + kept[:, CHUNK:], axis=0, keepdims=True)
                carried = twice(last) * carried + grown
            else:
                carried = grown
        else:
            drest = dright * vc
        dqs[c] = dq
        dks[c] = dk
        dbeta = drest[:, :CHUNK] + drest[:, CHUNK:] - m
        dbeta_ref[0, :, span] = jnp.sum(dbeta.T, axis=0, keepdims=True)
        lift = jnp.sum(side.T - tally, axis=0, keepdims=True)
        if edge is not None:
            lane = lax.broadcasted_iota(jnp.int32, (1, CHUNK), 1)
            lift = lift + jnp.where(lane == CHUNK - 1, jnp.sum(edge, axis=1, keepdims=True), 0.0)
        lift_ref[h, :, span] = lift
    dgain_ref[...] += dgain

    def spread(grad, ref, tap_ref, to_ref, dtap_ref):
        x, taps = ref[...].astype(F32), tap_ref[...]
        total = grad * taps[0:1]
        sums = [jnp.sum(grad * x, axis=0, keepdims=True)]
        for shift in range(1, CONV):
            masked = grad * wide(mask_ref[shift - 1], x.shape[1])
            sums.append(jnp.sum(masked * pltpu.roll(x, shift, 0), axis=0, keepdims=True))
            total = total + pltpu.roll(masked, rows - shift, 0) * taps[shift : shift + 1]
        to_ref[...] = total.astype(BF)
        dtap_ref[...] = jnp.concatenate(sums, axis=0)

    spread(jnp.concatenate(dqs, axis=0) * qslope, q_ref, tapq_ref, dq_ref, dtapq_ref)
    dk = jnp.concatenate(dks, axis=0)
    dk = kscale * (dk - kunit * jnp.sum(kunit * dk, axis=-1, keepdims=True))
    spread(dk * kslope, k_ref, tapk_ref, dk_ref, dtapk_ref)
    spread(jnp.concatenate(dvs, axis=0) * vslope, v_ref, tapv_ref, dv_ref, dtapv_ref)

    @pl.when(h == pl.num_programs(0) - 1)
    def _():
        heads = gamma_ref.shape[0]
        lane = lax.broadcasted_iota(jnp.int32, (heads, CHUNK), 1)
        for c in range(chunks):
            span = pl.ds(c * CHUNK, CHUNK)
            total = jnp.concatenate([lift_ref[i, :, span] for i in range(heads)], axis=0)
            step = 1
            while step < CHUNK:
                total = total + jnp.where(lane < CHUNK - step, pltpu.roll(total, CHUNK - step, 1), 0.0)
                step *= 2
            dgamma_ref[:, span] = total


def mixer_back(projected, at, seg, segrow, gamma, beta, taps, gain, out, fresh, inv, state, back, back_at, into):
    rows, width = projected.shape
    chunks, heads = rows // CHUNK, gamma.shape[0]
    given = [] if into is None else [into]
    return pl.pallas_call(
        back_kernel,
        grid=(heads,),
        in_specs=[
            columns(rows, HEAD, at),
            whole((rows, CHUNK)), whole((8, rows)), whole((heads, rows)), per_head(rows),
            columns(CONV, TAPS, at), whole((1, DV)),
            columns(rows, DV, 0), columns(rows, DV, 0),
            pl.BlockSpec((1, chunks, CHUNK, CHUNK), lambda h: (h, 0, 0, 0)),
            pl.BlockSpec((1, chunks, DK, DV), lambda h: (h, 0, 0, 0)),
            columns(rows, DV, back_at),
        ] + [pl.BlockSpec(memory_space=pl.ANY)] * len(given),
        out_specs=[
            columns(rows, HEAD, at), columns(CONV, TAPS, 0),
            whole((1, DV)), whole((heads, rows)), per_head(rows),
        ],
        out_shape=[
            jax.ShapeDtypeStruct((rows, width), BF),
            jax.ShapeDtypeStruct((CONV, heads * TAPS), F32),
            jax.ShapeDtypeStruct((1, DV), F32),
            jax.ShapeDtypeStruct((heads, rows), F32),
            jax.ShapeDtypeStruct((heads, 1, rows), F32),
        ],
        scratch_shapes=[
            pltpu.VMEM((CONV - 1, rows, CHUNK), F32),
            pltpu.VMEM((heads, 1, rows), F32),
            pltpu.VMEM((heads, 1, rows), F32),
        ],
        input_output_aliases={12: 0} if given else {},
        compiler_params=pltpu.CompilerParams(vmem_limit_bytes=32 * 2**20),
        cost_estimate=pl.CostEstimate(flops=heads * int(6e9), bytes_accessed=heads * int(5e6), transcendentals=0),
    )(projected, seg, segrow, gamma, beta[:, None], taps, gain, out, fresh, inv, state, back, *given)


TILE = 256


def ffn_in_kernel(x_ref, gate_w_ref, up_w_ref, gate_ref, up_ref, inner_ref):
    gate, up = dot_nn(x_ref[...], gate_w_ref[...]), dot_nn(x_ref[...], up_w_ref[...])
    gate_ref[...] = gate.astype(BF)
    up_ref[...] = up.astype(BF)
    inner_ref[...] = (gate * sigmoid(gate) * up).astype(BF)


def ffn_in(x, weight):
    rows, depth = x.shape
    width = weight.shape[1] // 2
    tiles = width // TILE
    return pl.pallas_call(
        ffn_in_kernel,
        grid=(tiles,),
        in_specs=[whole((rows, depth)), columns(depth, TILE, 0), columns(depth, TILE, tiles)],
        out_specs=[columns(rows, TILE, 0)] * 3,
        out_shape=[jax.ShapeDtypeStruct((rows, width), BF)] * 3,
        compiler_params=pltpu.CompilerParams(vmem_limit_bytes=32 * 2**20),
        cost_estimate=pl.CostEstimate(flops=4 * rows * depth * width, bytes_accessed=4 * depth * width, transcendentals=0),
    )(x, weight, weight)


def ffn_out_kernel(c_ref, gate_ref, up_ref, inner_ref, down_w_ref, gate_w_ref, up_w_ref, back_ref, down_ref, x_back_ref):
    @pl.when(pl.program_id(0) == 0)
    def _():
        down_ref[...] = jnp.zeros_like(down_ref)
        x_back_ref[...] = jnp.zeros_like(x_back_ref)

    inner_back = dot_nt(c_ref[...], down_w_ref[...])
    gate, up = gate_ref[...].astype(F32), up_ref[...].astype(F32)
    s = sigmoid(gate)
    gate_back = (inner_back * up * (s * (1.0 + gate * (1.0 - s)))).astype(BF)
    up_back = (inner_back * (gate * s)).astype(BF)
    back_ref[0] = gate_back
    back_ref[1] = up_back
    down_ref[...] += dot_nn(inner_ref[...], down_w_ref[...])
    x_back_ref[...] += dot_nt(gate_back, gate_w_ref[...]) + dot_nt(up_back, up_w_ref[...])


def ffn_out(cotangent, gate, up, inner, down_w, gate_up_w):
    rows, width = gate.shape
    depth = cotangent.shape[1]
    tiles = width // TILE
    return pl.pallas_call(
        ffn_out_kernel,
        grid=(tiles,),
        in_specs=[
            whole((rows, depth)),
            columns(rows, TILE, 0), columns(rows, TILE, 0), columns(rows, TILE, 0),
            pl.BlockSpec((TILE, depth), lambda h: (h, 0)),
            columns(depth, TILE, 0), columns(depth, TILE, tiles),
        ],
        out_specs=[pl.BlockSpec((2, rows, TILE), lambda h: (0, 0, h)), whole((rows, depth)), whole((rows, depth))],
        out_shape=[
            jax.ShapeDtypeStruct((2, rows, width), BF),
            jax.ShapeDtypeStruct((rows, depth), F32),
            jax.ShapeDtypeStruct((rows, depth), F32),
        ],
        compiler_params=pltpu.CompilerParams(vmem_limit_bytes=32 * 2**20),
        cost_estimate=pl.CostEstimate(flops=8 * rows * depth * width, bytes_accessed=6 * depth * width, transcendentals=0),
    )(cotangent, gate, up, inner, down_w, gate_up_w, gate_up_w)


SHIFTS = (1, 2, 3)


def place():
    rep = lax.axis_index("rep")
    core, x, y = rep % 2, (rep // 2) % 2, (rep // 4) % 2
    a = jnp.where(core == 0, x, y)
    b = jnp.where(core == 0, y, x)
    return core, a, b


def hop(value, kind):
    count = lax.axis_size("rep")
    if kind == "core":
        pairs = [(i, i ^ 1) for i in range(count)]
    elif kind == "first":
        pairs = [(i, i ^ (4 if i & 1 else 2)) for i in range(count)]
    elif kind == "second":
        pairs = [(i, i ^ (2 if i & 1 else 4)) for i in range(count)]
    else:
        pairs = [(i, i ^ kind) for i in range(count)]
    return lax.ppermute(value, "rep", pairs)


def shift(value, by):
    count = lax.axis_size("shard")
    return lax.ppermute(value, "shard", [(i, (i + by) % count) for i in range(count)])


def after(value, *others):
    if not others:
        return value
    return lax.optimization_barrier((value,) + others)[0]


def assemble_kernel(along, size, rows, cuts, at_ref, own_ref, *refs):
    pieces, whole_ref = refs[:-1], refs[-1]
    to = 0
    for start, width in cuts:
        whole_ref[pl.ds(pl.multiple_of(at_ref[0] * rows, 16), rows), to : to + width] = own_ref[:, start : start + width]
        to += width
    n = 1
    for piece in pieces:
        for slot in range(piece.shape[0]):
            block, part = at_ref[n], at_ref[n + 1]
            n += 2
            if along == 0:
                whole_ref[pl.ds(pl.multiple_of(block * rows + part * size, 16), size), :] = piece[slot]
            else:
                whole_ref[pl.ds(pl.multiple_of(block * rows, 16), rows), pl.ds(pl.multiple_of(part * size, 128), size)] = piece[slot]


class Gather:
    def __init__(self, weight, along, cuts=None, blocks=None):
        self.weight, self.along, self.blocks = weight, along, blocks
        self.cuts = cuts or [(0, weight.shape[1])]
        self.width = sum(width for _, width in self.cuts)
        self.size = (weight.shape[0], self.width)[along] // 8

    def deep(self, *tokens):
        core, a, b = place()
        part = core * 4 + a * 2 + b
        if self.blocks is None:
            mine = lax.dynamic_slice_in_dim(self.weight, part * self.size, self.size, self.along)
        else:
            mine = jnp.concatenate([pick(self.weight, n, 128, 1) for n in self.blocks(part)], axis=1)
        mine = after(mine, *tokens)
        self.raw = [shift(mine, by) for by in range(1, lax.axis_size("shard"))]

    def first(self, *tokens):
        count = len(self.raw)
        raw = lax.optimization_barrier(tuple(self.raw) + tokens)[:count]
        self.here = jnp.stack(raw)
        self.come = hop(self.here, "first")

    def second(self, *tokens):
        self.pair = jnp.concatenate([self.here, after(self.come, *tokens)])
        self.others = hop(self.pair, "second")
        self.pair_core = hop(self.pair, "core")

    def core(self, *tokens):
        self.others_in = after(self.others, *tokens)
        self.others_core = hop(self.others_in, "core")

    def full(self, *tokens):
        core, a, b = place()
        z, count = lax.axis_index("shard"), lax.axis_size("shard")
        part, other = core * 4 + a * 2 + b, (1 - core) * 4 + b * 2 + a
        blocks = [(z - by) % count for by in range(1, count)]
        at = [z]
        for home, flips in ((part, (0, 2)), (part, (1, 3)), (other, (0, 2)), (other, (1, 3))):
            for flip in flips:
                for block in blocks:
                    at += [block, home ^ flip]
        rows, width = self.weight.shape[0], self.width
        pieces = [self.pair, self.others_in, self.pair_core, after(self.others_core, *tokens)]
        return pl.pallas_call(
            functools.partial(assemble_kernel, self.along, self.size, rows, self.cuts),
            in_specs=[pl.BlockSpec(memory_space=pltpu.SMEM)] + [pl.BlockSpec(memory_space=pltpu.VMEM)] * 5,
            out_specs=pl.BlockSpec(memory_space=pltpu.VMEM),
            compiler_params=pltpu.CompilerParams(vmem_limit_bytes=48 * 2**20),
            out_shape=jax.ShapeDtypeStruct((rows * count, width), BF),
        )(jnp.stack(at).astype(jnp.int32), self.weight, *pieces)


def pick(value, at, size, axis):
    return lax.dynamic_slice_in_dim(value, at * size, size, axis)


def join(bit, mine, theirs, axis):
    return jnp.where(bit == 0, jnp.concatenate([mine, theirs], axis), jnp.concatenate([theirs, mine], axis))


class Total:
    def __init__(self, left, right):
        self.left, self.right = left, right
        self.count = lax.axis_size("shard")
        self.rows = left.shape[1] // self.count
        self.quarter = right.size // right.shape[-2] // 4

    def core(self, *tokens):
        core, a, b = place()
        half = 2 * self.quarter
        right = after(self.right, *tokens) if tokens else self.right
        if right.ndim == 3:
            self.own, other = (pick(right, n, 1, 0)[0] for n in (core, 1 - core))
        else:
            self.own, other = (pick(right, n, half, 1) for n in (core, 1 - core))
        self.given = dot_tn(self.left, other).astype(BF)
        self.got = hop(self.given, "core")
        return self.got

    def first(self, *tokens):
        core, a, b = place()
        self.got = after(self.got, *tokens)
        sent = dot_tn(self.left, pick(self.own, 1 - a, self.quarter, 1)) + pick(self.got, 1 - a, self.quarter, 1).astype(F32)
        self.sent = sent.astype(BF)
        self.got_first = hop(self.sent, "first")

    def second(self, *tokens):
        core, a, b = place()
        got_first = after(self.got_first, *tokens)
        kept = dot_tn(self.left, pick(self.own, a, self.quarter, 1)) + pick(self.got, a, self.quarter, 1).astype(F32)
        kept = (kept + got_first.astype(F32)).astype(BF).reshape(self.count, self.rows, self.quarter)
        self.axis = 2 if self.quarter % 256 == 0 else 1
        size = kept.shape[self.axis] // 2
        self.passed = pick(kept, 1 - b, size, self.axis)
        self.mine = pick(kept, b, size, self.axis)
        self.got_second = hop(self.passed, "second")

    def deep(self, *tokens):
        z = lax.axis_index("shard")
        kept = (self.mine.astype(F32) + after(self.got_second, *tokens).astype(F32)).astype(BF)
        extra = 8
        while extra < lax.axis_size("rep"):
            kept = (kept.astype(F32) + hop(kept, extra).astype(F32)).astype(BF)
            extra *= 2
        self.kept = kept
        self.raw = [shift(pick(kept, (z + by) % self.count, 1, 0)[0], by) for by in range(1, self.count)]

    def finish(self, *tokens):
        total = pick(self.kept, lax.axis_index("shard"), 1, 0)[0].astype(F32)
        for piece in lax.optimization_barrier(tuple(self.raw) + tokens)[: len(self.raw)]:
            total = total + piece.astype(F32)
        self.done = total.astype(BF)


def final_kernel(copies, at_ref, *refs):
    pieces, outs = refs[:8], refs[8:]
    n = 0
    for piece in pieces:
        for start, size, width, out, moving, fixed in copies:
            block = piece[start : start + size, :width].astype(F32)
            if moving == "both":
                rows = pl.ds(pl.multiple_of(at_ref[n] * size, 8), size)
                outs[out][rows, pl.ds(pl.multiple_of(at_ref[n + 1] * 128, 128), width)] = block
                n += 2
            else:
                outs[out][:, pl.ds(pl.multiple_of(at_ref[n] * 128, 128), width)] = block
                n += 1


class Spread:
    def __init__(self, done):
        self.done = done
        self.theirs = hop(done, "second")

    def first(self, *tokens):
        self.pair = jnp.stack([self.done, after(self.theirs, *tokens)])
        self.others = hop(self.pair, "first")

    def core(self, *tokens):
        self.four = jnp.concatenate([self.pair, after(self.others, *tokens)])
        self.over = hop(self.four, "core")

    def parts(self, *tokens):
        over = after(self.over, *tokens)
        return [self.four[n] for n in range(4)] + [over[n] for n in range(4)]


def part_numbers():
    core, a, b = place()
    home, away = core * 4 + a * 2 + b, (1 - core) * 4 + b * 2 + a
    return [home ^ n for n in range(4)] + [away ^ n for n in range(4)]


def finish_totals(pieces, copies, at, shapes):
    return pl.pallas_call(
        functools.partial(final_kernel, copies),
        in_specs=[pl.BlockSpec(memory_space=pltpu.SMEM)] + [pl.BlockSpec(memory_space=pltpu.VMEM)] * 8,
        out_specs=[pl.BlockSpec(memory_space=pltpu.VMEM)] * len(shapes),
        compiler_params=pltpu.CompilerParams(vmem_limit_bytes=48 * 2**20),
        out_shape=[jax.ShapeDtypeStruct(s, F32) for s in shapes],
    )(jnp.stack(at).astype(jnp.int32), *pieces)


def rms_scale(values, gain):
    return values * lax.rsqrt(jnp.mean(values * values, axis=-1, keepdims=True) + epsilon) * gain


def as_rows(x, count):
    flat = x.astype(F32).reshape(count, -1)
    return jnp.pad(flat, ((0, 0), (0, -flat.shape[1] % 1024))).reshape(count, -1, 128)


def from_rows(rows, shapes):
    found, start = [], 0
    for shape in shapes:
        size = math.prod(shape)
        deep = -(-size // 1024) * 8
        piece = rows[:, start : start + deep].reshape(rows.shape[0], -1)[:, :size]
        found.append(piece.reshape((rows.shape[0],) + shape))
        start += deep
    return found


def share_small(arrays, *tokens):
    count = lax.axis_size("shard")
    z = lax.axis_index("shard")
    flat = after(jnp.concatenate([as_rows(x, 1) for x in arrays], axis=1), *tokens)
    every = jnp.zeros((count,) + flat.shape[1:], F32)
    every = lax.dynamic_update_slice_in_dim(every, flat, z, 0)
    for by in range(1, count):
        every = lax.dynamic_update_slice_in_dim(every, shift(flat, by), (z - by) % count, 0)
    return from_rows(every, [x.shape for x in arrays])


class Small:
    def __init__(self, arrays):
        self.shapes = [x.shape[1:] for x in arrays]
        count, z = lax.axis_size("shard"), lax.axis_index("shard")
        flat = jnp.concatenate([as_rows(x, count) for x in arrays], axis=1)
        self.total = pick(flat, z, 1, 0)
        self.raw = [shift(pick(flat, (z + by) % count, 1, 0), by) for by in range(1, count)]
        self.step = 1

    def add(self, *tokens):
        for piece in lax.optimization_barrier(tuple(self.raw) + tokens)[: len(self.raw)]:
            self.total = self.total + piece
        if self.step < lax.axis_size("rep"):
            self.raw = [hop(self.total, self.step)]
            self.step *= 2
        else:
            self.raw = []

    def finish(self):
        while self.raw:
            self.add()
        return [x[0] for x in from_rows(self.total, self.shapes)]


def beside(blocks):
    return jnp.concatenate(list(blocks), axis=-1)


def parted(x):
    count = lax.axis_size("shard")
    return jnp.moveaxis(x.reshape(x.shape[:-1] + (count, -1)), -2, 0)


GROUPS = 2
STEPS = 4


def group_cuts(g):
    cuts = []
    for h in range(g * HEADS // GROUPS, (g + 1) * HEADS // GROUPS):
        cuts += [(h * DK, DK), (KEYS + h * DK, DK), (2 * KEYS + h * DV, DV), (2 * KEYS + VALS + h * DV, DV)]
    return cuts


def group_blocks(g, part):
    each, found = HEAD * HEADS // GROUPS // 8 // 128, []
    for n in range(each):
        block = (part + 8 * g) * each + n
        head, slot = block // (HEAD // 128), block % (HEAD // 128)
        to = jnp.where(slot < 2, slot * HEADS + head, 2 * HEADS + 2 * head + slot - 2)
        found.append(jnp.where(slot < 4, to, 4 * HEADS + 2 * head + slot - 4))
    return found


def mix_final_kernel(blocks, at_ref, *refs):
    for n, piece in enumerate(refs[:-1]):
        for m in range(blocks):
            to = pl.ds(pl.multiple_of(at_ref[n * blocks + m] * 128, 128), 128)
            refs[-1][:, to] = piece[:, m * 128 : (m + 1) * 128].astype(F32)


def finish_mix(pieces, blocks, at, shape):
    return pl.pallas_call(
        functools.partial(mix_final_kernel, blocks),
        in_specs=[pl.BlockSpec(memory_space=pltpu.SMEM)] + [pl.BlockSpec(memory_space=pltpu.VMEM)] * len(pieces),
        out_specs=pl.BlockSpec(memory_space=pltpu.VMEM),
        compiler_params=pltpu.CompilerParams(vmem_limit_bytes=48 * 2**20),
        out_shape=jax.ShapeDtypeStruct(shape, F32),
    )(jnp.stack(at).astype(jnp.int32), *pieces)


def body(
    hidden_in,
    segment_ids,
    norm_gains,
    w_mix_in,
    w_decay,
    decay_params,
    conv_weight,
    out_gain,
    w_mix_out,
    w_gate_up,
    w_down,
    cotangent,
):
    rows = hidden_in.shape[0]
    ga, gb = (
        Gather(w_mix_in, 1, group_cuts(g), functools.partial(group_blocks, g)) for g in range(GROUPS)
    )
    go, gu, gd = Gather(w_mix_out, 1), Gather(w_gate_up, 0), Gather(w_down, 1)
    ga.deep()
    ga.first()
    gb.deep(*ga.raw)
    ga.second(*gb.raw)
    go.deep(*gb.raw)
    ga.core(*go.raw)

    small = share_small([norm_gains, decay_params, conv_weight, out_gain[None], w_decay], ga.raw[0])
    gains, rates, taps, gain_row = (beside(x) for x in small[:4])
    decay_full = small[4].reshape(-1, 2 * HEADS).astype(BF)

    hidden = hidden_in.astype(F32)
    normed_one_f, norm_one_pull = jax.vjp(rms_scale, hidden, gains[0])
    normed_one = normed_one_f.astype(BF)
    logits = dot_nt(decay_full.T, normed_one)
    rate, bias = jnp.exp(rates[0])[:, None], rates[1][:, None]
    gamma = -rate * jax.nn.softplus(logits[:HEADS] + bias)
    beta = jax.nn.sigmoid(logits[HEADS:])
    seg = jnp.broadcast_to(segment_ids[:, None], (rows, CHUNK))
    segrow = jnp.broadcast_to(segment_ids[None], (8, rows))
    cuts = (taps[:, :KEYS], taps[:, KEYS : 2 * KEYS], taps[:, 2 * KEYS :])
    by_head = jnp.concatenate([x.reshape(CONV, HEADS, -1) for x in cuts], axis=2).reshape(CONV, -1)
    tap_groups = jnp.split(by_head, GROUPS, axis=1)
    heads = HEADS // STEPS

    mix_in = [ga.full(), None]
    gb.first(mix_in[0])
    projected = [dot_nn(normed_one, mix_in[0]).astype(BF), None]
    gb.second(projected[0])
    gu.deep(mix_in[0])
    kept = []

    def mix(n, *tokens):
        g, at = n * GROUPS // STEPS, n % (STEPS // GROUPS) * heads
        span = slice(n * heads, (n + 1) * heads)
        gate = after(gamma[span], *tokens) if tokens else gamma[span]
        kept.append(mixer(projected[g], at, seg, segrow, gate, beta[span], tap_groups[g], gain_row))
        return kept[-1][0]

    done = mix(0)
    gb.core(done)
    done = mix(1, gu.raw[0])
    mix_in[1] = gb.full(done)
    go.first(done)
    projected[1] = dot_nn(after(normed_one, done, gu.raw[1]), mix_in[1]).astype(BF)
    go.second(projected[1])
    gu.first(projected[1])
    gd.deep(projected[1], *gu.raw)
    done = mix(2, gu.here, go.pair)
    gu.second(done)
    go.core(done)
    done = mix(3, gu.pair, gd.raw[0])
    gd.first(done)
    mix_out = go.full()
    mixed_out = jnp.concatenate([x[0] for x in kept], axis=1)
    residual = hidden + dot_nn(mixed_out, mix_out)
    normed_two_f, norm_two_pull = jax.vjp(rms_scale, residual, gains[1])
    normed_two = normed_two_f.astype(BF)
    gu.core(normed_two)
    gate_up_full = gu.full()
    gd.second(gate_up_full)
    gate, up, inner = ffn_in(after(normed_two, gd.pair), gate_up_full)
    gd.core(inner)
    down_full = gd.full()
    t_down = Total(inner, cotangent)
    t_down.core()
    gate_up_back, down, normed_two_back = ffn_out(
        after(cotangent, t_down.given), gate, up, inner, down_full, gate_up_full
    )
    t_gu = Total(normed_two, gate_up_back)
    t_gu.core()
    t_down.first(t_gu.given)
    result = (residual + down).astype(BF)
    residual_part, gain_two = norm_two_pull(after(normed_two_back, t_down.sent))
    t_gu.first(gain_two)
    residual_back = cotangent.astype(F32) + residual_part
    branch_back = after(residual_back.astype(BF), t_gu.sent)
    t_out = Total(mixed_out, branch_back)
    t_out.core()
    mixed_back = dot_nt(branch_back, mix_out).astype(BF)

    backs = []

    def mix_back(n, *tokens):
        g, at = n * GROUPS // STEPS, n % (STEPS // GROUPS) * heads
        span = slice(n * heads, (n + 1) * heads)
        gate = after(gamma[span], *tokens)
        into = backs[-1][0] if at else None
        backs.append(
            mixer_back(
                projected[g], at, seg, segrow, gate, beta[span], tap_groups[g], gain_row, *kept[n][1:], mixed_back, n * heads, into
            )
        )
        return backs[-1][0]

    done = mix_back(0, t_gu.sent, t_out.given)
    t_out.first(done)
    t_down.second(done)
    done = mix_back(1, t_out.sent, t_down.passed)
    back_a = done
    t_a = Total(normed_one, back_a)
    t_a.core(done)
    t_down.deep(done)
    done = mix_back(2, t_a.given, t_down.kept)
    t_gu.second(done)
    t_a.first(t_gu.passed)
    t_out.second(t_a.sent)
    done = mix_back(3, t_a.sent, t_out.passed)
    t_down.finish(done)
    back_b = done
    t_b = Total(normed_one, back_b)
    t_b.core(done)
    t_gu.deep(t_b.given)
    t_out.deep(t_gu.kept)
    dgain = sum(x[2] for x in backs)
    dgamma = jnp.concatenate([x[3] for x in backs], axis=0)
    dbeta = jnp.concatenate([x[4][:, 0] for x in backs], axis=0)
    slope = -dgamma * rate * jax.nn.sigmoid(logits[:HEADS] + bias)
    logits_back = jnp.concatenate([slope, dbeta * beta * (1.0 - beta)], axis=0).astype(BF)
    grad_rates = jnp.stack([jnp.sum(dgamma * gamma, axis=1), jnp.sum(slope, axis=1)])
    by_head = jnp.concatenate([x[1] for x in backs], axis=1).reshape(CONV, HEADS, TAPS)
    cuts = (by_head[:, :, :DK], by_head[:, :, DK : 2 * DK], by_head[:, :, 2 * DK :])
    grad_taps = jnp.concatenate([x.reshape(CONV, -1) for x in cuts], axis=1)
    grad_decay = lax.dot_general(normed_one, logits_back, (((0,), (1,)), ((), ())), preferred_element_type=F32)
    t_b.first()
    near = lax.dot_general(logits_back, decay_full, (((0,), (1,)), ((), ())), preferred_element_type=F32)
    near = near + dot_nt(after(back_a, t_b.sent), mix_in[0]) + dot_nt(back_b, mix_in[1])
    t_a.second(near)
    hidden_part, gain_one = norm_one_pull(after(near, t_a.passed))
    grad_in = residual_back + hidden_part
    t_b.second(gain_one)
    t_a.deep(t_b.passed)
    t_gu.finish(t_b.passed)
    t_out.finish(t_b.passed)
    count = lax.axis_size("shard")
    small_total = Small([
        parted(jnp.stack([gain_one, gain_two])),
        grad_decay.reshape(count, -1, 2 * HEADS),
        parted(grad_rates),
        parted(grad_taps),
        parted(dgain[0]),
    ])
    numbers = part_numbers()
    wide = t_gu.done.shape[1] // 128
    merged = jnp.concatenate(
        [t_down.done, t_out.done] + [t_gu.done[:, n * 128 : (n + 1) * 128] for n in range(wide)]
    )
    s_rest = Spread(merged)
    t_b.deep(s_rest.done)
    small_total.add(t_b.kept)
    s_rest.first(t_b.raw[0])
    t_a.finish(s_rest.pair)
    t_b.finish(s_rest.pair)
    s_mix = Spread(jnp.concatenate([t_a.done, t_b.done], axis=1))
    small_total.add(s_mix.done)
    s_rest.core(s_mix.done)
    s_mix.first(s_rest.four)
    small_total.add(s_mix.pair)
    copies, at, start = [], [], 0
    for out, deep in enumerate((t_down.rows, t_out.rows)):
        copies.append((start, deep, 128, out, "columns", 0))
        start += deep
    for n in range(wide):
        copies.append((start, t_gu.rows // 2, 128, 2, "both", n))
        start += t_gu.rows // 2
    for part in numbers:
        at += [part, part]
        for n in range(wide):
            at += [part % 2, part // 2 * wide + n]
    grad_down, grad_mix_out, grad_gate_up = finish_totals(
        s_rest.parts(s_mix.pair), copies, at, [w_down.shape, w_mix_out.shape, w_gate_up.shape]
    )
    s_mix.core(grad_down)
    small_total.add(s_mix.four)
    parts = small_total.finish()
    each = t_a.done.shape[1] // 128
    copies, at = [], []
    for part in numbers:
        for g in range(GROUPS):
            at += group_blocks(g, part)
    pieces = s_mix.parts()
    grad_mix_in = finish_mix(pieces, GROUPS * each, at, w_mix_in.shape)
    return (
        result,
        grad_in,
        parts[0],
        grad_mix_in,
        parts[1],
        parts[2],
        parts[3],
        parts[4],
        grad_mix_out,
        grad_gate_up,
        grad_down,
    )


def solution(mesh):
    rows, columns_, both = P("shard", None), P(None, "shard"), P(("rep", "shard"), None)
    return jax.shard_map(
        body,
        mesh=mesh,
        in_specs=(both, P(("rep", "shard")), columns_, rows, rows, columns_, columns_, P("shard"), rows, rows, rows, both),
        out_specs=(both, both, columns_, rows, rows, columns_, columns_, P("shard"), rows, rows, rows),
        check_vma=False,
    )
```
